32 devices in a mesh: slab: 2 (over x), outer: 2 (over core), inner: 8 (over z, y).
Axes of the slice: x: 2, y: 2, z: 4, core: 2. Of those that a mesh axis runs over, the one named last changes fastest.
Arguments:
- x_stream: bfloat16 [8192, 8192], P(('slab', 'outer', 'inner')), parts along dimension 0, may hold values from -6 to 6
- b_stream: bfloat16 [8192, 1024], P(('slab', 'outer', 'inner')), parts along dimension 0, may hold values from -6 to 6
- c_stream: bfloat16 [8192, 1024], P(('slab', 'outer', 'inner')), parts along dimension 0, may hold values from -6 to 6
- dt_input: bfloat16 [8192, 128], P(('slab', 'outer', 'inner')), parts along dimension 0, may hold values from -20 to 16, as said below
- decay_log: float32 [256], P('slab'), parts along dimension 0, may hold values from -3.5 to 0.6
- skip_weight: float32 [128], replicated, may hold values from 0.1 to 1.9
- conv_weight: bfloat16 [4, 10240], replicated, may hold values from -3 to 3
Outputs:
- scan_out: bfloat16 [8192, 8192], P(('slab', 'outer', 'inner')), parts along dimension 0
The draws below stay inside these ranges and needn't reach their ends.
There are 2 independent parts, one for each index of `slab`. The reference program is written for one: setup_inputs(seed, part) draws one part's arguments, and reference() takes and returns one part's arrays. A program takes and returns all parts, laid end to end along the dimension named above; an argument that names none is the same for every part. Nothing has to cross between parts.
Inputs may be any that keep to these rules, and one draw needn't show every extreme that they name: `dt_input`: the softplus inverse of a positive time step.
All inputs are finite; a program needn't handle non-finite values.
Results may differ from the reference program's by a relative error of at most 0.0039.
Values may be sent and summed in bfloat16 or wider, within the bound.
No kernel may reach another device: no remote copies, remote signals or barrier semaphores. Data moves between devices by JAX's collectives and lax.ppermute only.
A program may use at most 320 MiB of HBM per device.

```python
import jax
import jax.numpy as jnp
from jax import lax

H = 128
P_SIZE = 64
N = 128
G = 8
KERNEL_TAPS = 4
TOK_DEV = 256
SPAN = 256
SLAB_TOKENS = 4096


def decay_layout(key, slow_fraction):
    random_subkeys = jax.random.split(key, 7)
    slow_heads = jax.random.uniform(random_subkeys[0], (H,)) < slow_fraction
    spread = jnp.exp(jax.random.uniform(random_subkeys[1], (H,), jnp.float32, jnp.log(0.5), jnp.log(2.0)))
    memory = jnp.exp(jax.random.uniform(random_subkeys[2], (H,), jnp.float32, jnp.log(16.0), jnp.log(8.0 * SPAN)))
    reach_gain = jnp.exp(jax.random.uniform(random_subkeys[4], (H,), jnp.float32, jnp.log(0.6), jnp.log(2.0)))
    baseline_step = jnp.where(slow_heads, 1.5 * spread / SLAB_TOKENS, reach_gain / memory)
    chain_rate = jnp.exp(jax.random.uniform(random_subkeys[3], (H,), jnp.float32, jnp.log(0.1), jnp.log(0.8)))
    decay_speeds = jnp.where(slow_heads, chain_rate / (SLAB_TOKENS * baseline_step), 1.0 / reach_gain)
    spurt_groups = jax.random.randint(random_subkeys[5], (3,), 0, SLAB_TOKENS)
    loss_values = jax.random.uniform(random_subkeys[6], (3, H), jnp.float32, 0.22, 0.5)
    spurt_steps = loss_values / decay_speeds[None, :]
    return (decay_speeds, baseline_step, spurt_groups, spurt_steps)


def draw_decay_log(key, part):
    slow_fraction = 0.5
    decay_speeds, baseline_step, spurt_groups, spurt_steps = decay_layout(key, slow_fraction)
    return jnp.log(decay_speeds).astype(jnp.float32)


def draw_dt_input(key, part):
    slow_fraction = 0.5
    decay_speeds, baseline_step, spurt_groups, spurt_steps = decay_layout(key, slow_fraction)
    key = jax.random.fold_in(key, 7)
    block_key, token_key = jax.random.split(key)
    block_factor = jnp.exp(jax.random.uniform(block_key, (SLAB_TOKENS // TOK_DEV, 1, 1), jnp.float32, jnp.log(0.5), jnp.log(2.0)))
    block_factor = jnp.broadcast_to(block_factor, (SLAB_TOKENS // TOK_DEV, TOK_DEV, H)).reshape(SLAB_TOKENS, H)
    token_factor = jnp.exp(jax.random.uniform(token_key, (SLAB_TOKENS, H), jnp.float32, jnp.log(0.6), jnp.log(1.6)))
    step_widths = baseline_step[None, :] * token_factor * block_factor
    token_positions = jnp.arange(SLAB_TOKENS)[:, None]
    for spurt_index in range(3):
        step_widths = jnp.where(token_positions == spurt_groups[spurt_index], spurt_steps[spurt_index][None, :], step_widths)
    inverse = step_widths + jnp.log(-jnp.expm1(-step_widths))
    return inverse.astype(jnp.bfloat16)


def draw_b_stream(key, part):
    decay_speeds, baseline_step, spurt_groups, spurt_steps = decay_layout(key, 0.5)
    key = jax.random.fold_in(key, 13)
    normal_key, period_key, phase_key = jax.random.split(key, 3)
    normal_part = jnp.clip(jax.random.normal(normal_key, (SLAB_TOKENS, G * N), jnp.float32), -6.0, 6.0)
    period = jax.random.randint(period_key, (), SPAN, 2 * SPAN + 1)
    phase = jax.random.uniform(phase_key, (), jnp.float32, 0.0, 6.283185307179586)
    index_positions = jnp.arange(SLAB_TOKENS, dtype=jnp.int32)
    fraction = (index_positions % period).astype(jnp.float32) / period.astype(jnp.float32)
    envelope = jnp.exp(0.6 * jnp.sin(6.283185307179586 * fraction + phase))[:, None]
    token_positions = index_positions[:, None]
    factor = jnp.ones((SLAB_TOKENS, 1), jnp.float32)
    for spurt_index in range(3):
        nearby_mask = (token_positions <= spurt_groups[spurt_index]) & (token_positions >= spurt_groups[spurt_index] - (KERNEL_TAPS - 1))
        factor = jnp.where(nearby_mask, 0.001, factor)
    shaped = jnp.clip(normal_part * envelope, -6.0, 6.0)
    return (shaped * factor).astype(jnp.bfloat16)


def block_levels(stream_key, shape, cuts, least, largest):
    factor_of, own = 1.0, jax.random.fold_in(stream_key, 6)
    for axis_at, shards_of in cuts:
        steps = jnp.exp(jax.random.uniform(jax.random.fold_in(own, axis_at), (shards_of,), jnp.float32, least / len(cuts), largest / len(cuts)))
        factor_of = factor_of * jnp.repeat(steps, shape[axis_at] // shards_of).reshape([-1 if axis == axis_at else 1 for axis in range(len(shape))])
    return factor_of


def scatter_about(key, extent, deviation, limit, cuts=(), held_as=jnp.bfloat16):
    entries = jax.random.normal(key, extent, jnp.float32) * deviation
    if len(cuts) > 0:
        entries = block_levels(key, extent, cuts, -0.22, 0.18) * entries
    return jnp.clip(entries, min=-limit, max=limit).astype(held_as)


def setup_inputs(seed: int = 0, part: int = 0) -> dict:
    key_list = jax.random.split(jax.random.key(seed), 8)
    own_keys = jax.random.split(jax.random.fold_in(key_list[7], part), 8)
    return {
        "x_stream": scatter_about(own_keys[0], (SLAB_TOKENS, H * P_SIZE), 1.0, 6.0, ((0, 16),)),
        "b_stream": draw_b_stream(jax.random.fold_in(jax.random.fold_in(key_list[7], part), 71), part),
        "c_stream": scatter_about(own_keys[2], (SLAB_TOKENS, G * N), 1.0, 6.0, ((0, 16),)),
        "dt_input": draw_dt_input(jax.random.fold_in(jax.random.fold_in(key_list[7], part), 71), part),
        "decay_log": draw_decay_log(jax.random.fold_in(jax.random.fold_in(key_list[7], part), 71), part),
        "skip_weight": jnp.clip(1.0 + 0.18 * jax.random.normal(key_list[5], (H,), jnp.float32), 0.1, 1.9),
        "conv_weight": scatter_about(key_list[6], (KERNEL_TAPS, H * P_SIZE + 2 * G * N), KERNEL_TAPS ** -0.5, 3.0),
    }


def rounded(values):
    return lax.optimization_barrier(values.astype(jnp.bfloat16)).astype(jnp.float32)


def reference(x_stream, b_stream, c_stream, dt_input, decay_log, skip_weight, conv_weight):
    value_cols = H * P_SIZE
    state_cols = G * N
    heads_group = H // G
    raw_cols = jnp.concatenate([x_stream, b_stream, c_stream], axis=1)
    padded = jnp.concatenate([jnp.zeros((KERNEL_TAPS - 1, raw_cols.shape[1]), raw_cols.dtype), raw_cols], axis=0)
    kernel = conv_weight.astype(jnp.float32)
    decay_speeds = -jnp.exp(decay_log.astype(jnp.float32))
    step_all = jax.nn.softplus(dt_input.astype(jnp.float32))
    skip_gain = skip_weight.astype(jnp.float32)
    token_positions = jnp.arange(SPAN)
    causal = token_positions[:, None] >= token_positions[None, :]

    def one_block(carry_state, block_index):
        first_row = (block_index * SPAN).astype(jnp.int32)
        window = lax.dynamic_slice_in_dim(padded, first_row, SPAN + KERNEL_TAPS - 1, 0).astype(jnp.float32)
        mixed_conv = kernel[0] * window[0:SPAN]
        for offset in range(1, KERNEL_TAPS):
            mixed_conv = mixed_conv + kernel[offset] * window[offset:offset + SPAN]
        conv_out = rounded(jax.nn.silu(mixed_conv))
        values = conv_out[:, :value_cols].reshape(SPAN, H, P_SIZE)
        inputs_b = conv_out[:, value_cols:value_cols + state_cols].reshape(SPAN, G, N)
        inputs_c = conv_out[:, value_cols + state_cols:].reshape(SPAN, G, N)
        step_widths = lax.dynamic_slice_in_dim(step_all, first_row, SPAN, 0)
        cumul = jnp.cumsum(step_widths * decay_speeds[None, :], axis=0)
        scores = jnp.einsum('tgn,sgn->gts', inputs_c, inputs_b)
        scores_heads = jnp.repeat(scores, heads_group, axis=0)
        cum_heads = cumul.T
        gaps = cum_heads[:, :, None] - cum_heads[:, None, :]
        decays = jnp.where(causal, jnp.exp(jnp.where(causal, gaps, 0.0)), 0.0)
        mixing = rounded(scores_heads * decays * step_widths.T[:, None, :])
        inside = jnp.einsum('hts,shp->thp', mixing, values)
        block_end = cumul[-1]
        to_end = jnp.exp(block_end[None, :] - cumul) * step_widths
        b_heads = jnp.repeat(inputs_b, heads_group, axis=1)
        weighted = rounded(b_heads * to_end[:, :, None])
        block_state = jnp.einsum('shn,shp->hnp', weighted, values)
        c_heads = jnp.repeat(inputs_c, heads_group, axis=1)
        carried = jnp.einsum('thn,hnp->thp', c_heads, rounded(carry_state)) * jnp.exp(cumul)[:, :, None]
        output = (inside + carried + skip_gain[None, :, None] * values).astype(jnp.bfloat16)
        next_state = jnp.exp(block_end)[:, None, None] * carry_state + block_state
        return next_state, output.reshape(SPAN, value_cols)

    start_state = jnp.zeros((H, N, P_SIZE), jnp.float32)
    final_state, outputs = lax.scan(one_block, start_state, jnp.arange(SLAB_TOKENS // SPAN, dtype=jnp.int32))
    return outputs.reshape(SLAB_TOKENS, value_cols)
```

```python
import jax
import jax.numpy as jnp
from jax import lax
from jax.experimental import pallas as pl
from jax.experimental.pallas import tpu as pltpu
from jax.sharding import PartitionSpec as P

H = 128
P_SIZE = 64
N = 128
G = 8
KERNEL_TAPS = 4
SPAN = 256

HEADS = H // G
COLS = HEADS * P_SIZE
HALF = N // 2
RIM = KERNEL_TAPS - 1
PAD = 8
LOG2E = 1.4426950408889634
VMEM = 48 * 1024 * 1024
F32 = jnp.float32
BF16 = jnp.bfloat16
CHUNKS = (2, 2, 2, 2)


def params():
    return pltpu.CompilerParams(vmem_limit_bytes=VMEM)


def cost(us, moved):
    return pl.CostEstimate(flops=int(us * 6e8), bytes_accessed=moved, transcendentals=0)


def steps_body(dt_ref, decay_ref, cols_ref, rows_ref, to_end_ref, from_start_ref, last_ref):
    raw = dt_ref[...].astype(F32)
    dt = jnp.maximum(raw, 0.0) + jnp.log1p(jnp.exp(-jnp.abs(raw)))
    step = dt * (-jnp.exp(decay_ref[...]))
    row = lax.broadcasted_iota(jnp.int32, (SPAN, SPAN), 0)
    col = lax.broadcasted_iota(jnp.int32, (SPAN, SPAN), 1)
    tri = jnp.where(row >= col, 1.0, 0.0).astype(F32)
    cum = jnp.dot(tri, step, precision=lax.Precision.HIGHEST, preferred_element_type=F32)
    last = cum[SPAN - 1 :, :]
    last_ref[...] = last
    rows_ref[...] = jnp.transpose((cum - jnp.log(dt)) * LOG2E)
    to_end = jnp.exp(last - cum) * dt
    from_start = jnp.exp(cum)
    scaled = cum * LOG2E
    for group in range(G):
        lo = group * HEADS
        cols_ref[group] = scaled[:, lo : lo + HEADS]
        for value, ref in ((to_end, to_end_ref), (from_start, from_start_ref)):
            part = value[:, lo : lo + HEADS]
            high = part.astype(BF16)
            low = (part - high.astype(F32)).astype(BF16)
            ref[group] = jnp.concatenate([high, low], axis=1)


def time_steps(dt_input, decay_log):
    return pl.pallas_call(
        steps_body,
        out_shape=(
            jax.ShapeDtypeStruct((G, SPAN, HEADS), F32),
            jax.ShapeDtypeStruct((H, SPAN), F32),
            jax.ShapeDtypeStruct((G, SPAN, 2 * HEADS), BF16),
            jax.ShapeDtypeStruct((G, SPAN, 2 * HEADS), BF16),
            jax.ShapeDtypeStruct((1, H), F32),
        ),
        compiler_params=params(),
        cost_estimate=cost(2.0, 1 << 20),
        name="time_steps",
    )(dt_input, decay_log.reshape(1, H))


def convolved(ref, rim_ref, kernel_ref, scratch):
    kernel = kernel_ref[...].astype(F32) * 0.5
    width = ref.shape[1]
    parts = []
    for lo in range(0, width, 128):
        sl = slice(lo, lo + 128)
        scratch[PAD - RIM : PAD, :] = rim_ref[:, sl].astype(F32)
        scratch[PAD : PAD + SPAN, :] = ref[:, sl].astype(F32)
        half = kernel[RIM : RIM + 1, sl] * scratch[PAD : PAD + SPAN, :]
        for tap in range(RIM):
            first = PAD - RIM + tap
            half = half + kernel[tap : tap + 1, sl] * scratch[first : first + SPAN, :]
        parts.append((half + half * jnp.tanh(half)).astype(BF16))
    return parts


def states_body(
    side_ref,
    x_ref,
    b_ref,
    c_ref,
    rim_x_ref,
    rim_b_ref,
    rim_c_ref,
    kernel_x_ref,
    kernel_b_ref,
    kernel_c_ref,
    to_end_ref,
    spread_ref,
    values_ref,
    conv_b_ref,
    conv_c_ref,
    keep_ref,
    send_ref,
    scratch,
):
    (conv_b,) = convolved(b_ref, rim_b_ref, kernel_b_ref, scratch)
    (conv_c,) = convolved(c_ref, rim_c_ref, kernel_c_ref, scratch)
    conv_b_ref[...] = conv_b
    conv_c_ref[...] = conv_c
    parts = convolved(x_ref, rim_x_ref, kernel_x_ref, scratch)
    for at, part in enumerate(parts):
        values_ref[:, at * 128 : (at + 1) * 128] = part
    gain = jnp.dot(to_end_ref[0], spread_ref[...], preferred_element_type=F32)
    weighted = (values_ref[...].astype(F32) * gain).astype(BF16)
    state = lax.dot_general(
        conv_b, weighted, (((0,), (0,)), ((), ())), preferred_element_type=F32
    ).astype(BF16)
    upper = side_ref[0] == 1
    top, bottom = state[:HALF], state[HALF:]

    @pl.when(upper)
    def _():
        keep_ref[0] = bottom
        send_ref[0] = top

    @pl.when(jnp.logical_not(upper))
    def _():
        keep_ref[0] = top
        send_ref[0] = bottom


def end_states(first, count, side, x, b, c, rim, conv_weight, to_end, spread):
    def cols(offset):
        return lambda i: (0, offset + first + i)

    def own(i):
        return (0, i)

    def lead(i):
        return (first + i, 0, 0)

    def lead_own(i):
        return (i, 0, 0)

    b_at, c_at = H * P_SIZE // N, H * P_SIZE // N + G
    return pl.pallas_call(
        states_body,
        grid=(count,),
        in_specs=[
            pl.BlockSpec(memory_space=pltpu.SMEM),
            pl.BlockSpec((SPAN, COLS), cols(0)),
            pl.BlockSpec((SPAN, N), cols(0)),
            pl.BlockSpec((SPAN, N), cols(0)),
            pl.BlockSpec((RIM, COLS), cols(0)),
            pl.BlockSpec((RIM, N), cols(b_at)),
            pl.BlockSpec((RIM, N), cols(c_at)),
            pl.BlockSpec((KERNEL_TAPS, COLS), cols(0)),
            pl.BlockSpec((KERNEL_TAPS, N), cols(b_at)),
            pl.BlockSpec((KERNEL_TAPS, N), cols(c_at)),
            pl.BlockSpec((1, SPAN, 2 * HEADS), lead),
            pl.BlockSpec((2 * HEADS, COLS), lambda i: (0, 0)),
        ],
        out_specs=[
            pl.BlockSpec((SPAN, COLS), own),
            pl.BlockSpec((SPAN, N), own),
            pl.BlockSpec((SPAN, N), own),
            pl.BlockSpec((1, HALF, COLS), lead_own),
            pl.BlockSpec((1, HALF, COLS), lead_own),
        ],
        out_shape=[
            jax.ShapeDtypeStruct((SPAN, count * COLS), BF16),
            jax.ShapeDtypeStruct((SPAN, count * N), BF16),
            jax.ShapeDtypeStruct((SPAN, count * N), BF16),
            jax.ShapeDtypeStruct((count, HALF, COLS), BF16),
            jax.ShapeDtypeStruct((count, HALF, COLS), BF16),
        ],
        scratch_shapes=[pltpu.VMEM((PAD + SPAN, 128), F32)],
        compiler_params=params(),
        cost_estimate=cost(1.2 * count, count << 20),
        name="end_states",
    )(side, x, b, c, rim, rim, rim, conv_weight, conv_weight, conv_weight, to_end, spread)


def inside_body(values_ref, b_ref, c_ref, cols_ref, rows_ref, skip_ref, part_ref):
    half = SPAN // 2
    scores = lax.dot_general(
        c_ref[...], b_ref[...], (((1,), (1,)), ((), ())), preferred_element_type=F32
    )
    row = lax.broadcasted_iota(jnp.int32, (half, half), 0)
    col = lax.broadcasted_iota(jnp.int32, (half, half), 1)
    causal = row >= col
    lane = lax.broadcasted_iota(jnp.int32, (half, 2 * P_SIZE), 1)
    first_head = lane < P_SIZE
    cols = cols_ref[0]
    rows = rows_ref[...]
    corner, below, later = scores[:half, :half], scores[half:, :half], scores[half:, half:]
    for pair in range(HEADS // 2):
        upper, lower = [], []
        for head in (2 * pair, 2 * pair + 1):
            at_t = cols[:, head : head + 1]
            at_s = rows[head : head + 1, :]
            e = jnp.exp2(at_t[:half] - at_s[:, :half])
            upper.append(jnp.where(causal, corner * e, 0.0).astype(BF16))
            e = jnp.exp2(at_t[half:] - at_s[:, :half])
            left = (below * e).astype(BF16)
            e = jnp.exp2(at_t[half:] - at_s[:, half:])
            right = jnp.where(causal, later * e, 0.0).astype(BF16)
            lower.append(jnp.concatenate([left, right], axis=1))
        sl = slice(pair * 2 * P_SIZE, (pair + 1) * 2 * P_SIZE)
        values = values_ref[:, sl]
        skip = skip_ref[:, sl]
        for lo, mix, depth in ((0, upper, half), (half, lower, SPAN)):
            both = jnp.dot(
                jnp.concatenate(mix, axis=0), values[:depth], preferred_element_type=F32
            )
            inside = jnp.where(first_head, both[:half], both[half:])
            part_ref[lo : lo + half, sl] = inside + skip * values[lo : lo + half].astype(F32)


def inside_block(first, count, values, conv_b, conv_c, cols, rows, skip):
    def own(i):
        return (0, i)

    return pl.pallas_call(
        inside_body,
        grid=(count,),
        in_specs=[
            pl.BlockSpec((SPAN, COLS), own),
            pl.BlockSpec((SPAN, N), own),
            pl.BlockSpec((SPAN, N), own),
            pl.BlockSpec((1, SPAN, HEADS), lambda i: (first + i, 0, 0)),
            pl.BlockSpec((HEADS, SPAN), lambda i: (first + i, 0)),
            pl.BlockSpec((1, COLS), lambda i: (0, first + i)),
        ],
        out_specs=pl.BlockSpec((SPAN, COLS), own),
        out_shape=jax.ShapeDtypeStruct((SPAN, count * COLS), F32),
        compiler_params=params(),
        cost_estimate=cost(1.6 * count, count << 20),
        name="inside_block",
    )(values, conv_b, conv_c, cols, rows, skip)


def carried_body(*refs):
    side_ref, c_ref, part_ref, keep_ref, got_ref, from_start_ref, spread_ref = refs[:7]
    out_ref = refs[-1]
    upper = side_ref[0] == 1
    keep, got = keep_ref[0], got_ref[0]
    carry = jnp.concatenate(
        [jnp.where(upper, got, keep), jnp.where(upper, keep, got)], axis=0
    )
    gain = jnp.dot(from_start_ref[0], spread_ref[...], preferred_element_type=F32)
    carried = jnp.dot(c_ref[...], carry, preferred_element_type=F32)
    out_ref[...] = (part_ref[...] + carried * gain).astype(BF16)


def with_carry(first, count, side, conv_c, part, keep, got, from_start, spread, out):
    def own(i):
        return (0, i)

    def lead_own(i):
        return (i, 0, 0)

    given = [] if out is None else [out]
    return pl.pallas_call(
        carried_body,
        grid=(count,),
        in_specs=[
            pl.BlockSpec(memory_space=pltpu.SMEM),
            pl.BlockSpec((SPAN, N), own),
            pl.BlockSpec((SPAN, COLS), own),
            pl.BlockSpec((1, HALF, COLS), lead_own),
            pl.BlockSpec((1, HALF, COLS), lead_own),
            pl.BlockSpec((1, SPAN, 2 * HEADS), lambda i: (first + i, 0, 0)),
            pl.BlockSpec((2 * HEADS, COLS), lambda i: (0, 0)),
        ]
        + [pl.BlockSpec(memory_space=pl.ANY)] * len(given),
        out_specs=pl.BlockSpec((SPAN, COLS), lambda i: (0, first + i)),
        out_shape=jax.ShapeDtypeStruct((SPAN, H * P_SIZE), BF16),
        input_output_aliases={7: 0} if given else {},
        compiler_params=params(),
        cost_estimate=cost(0.7 * count, count << 20),
        name="with_carry",
    )(side, conv_c, part, keep, got, from_start, spread, *given)


def swap(value, axis, pairs):
    both = [(a, b) for a, b in pairs] + [(b, a) for a, b in pairs]
    return lax.ppermute(value, axis, both)


def gathered_logs(last, y_pairs, z_pairs, far_pairs):
    at = lax.axis_index("inner")
    rows = last
    for bit, pairs in ((1, y_pairs), (2, z_pairs), (4, far_pairs)):
        other = swap(rows, "inner", pairs)
        low = (at & bit) == 0
        rows = jnp.concatenate(
            [jnp.where(low, rows, other), jnp.where(low, other, rows)], axis=0
        )
    other = swap(rows, "outer", [(0, 1)])
    low = lax.axis_index("outer") == 0
    return jnp.stack([jnp.where(low, rows, other), jnp.where(low, other, rows)])


def enter_by_swaps(last, kept, sent):
    size = lax.axis_size("inner")
    y_pairs = [(i, i + 1) for i in range(0, size, 2)]
    z_pairs = [(i, i + 2) for i in range(size) if i & 2 == 0]
    mid_pairs = [(2, 4), (3, 5)]
    far_pairs = [(i, i + 4) for i in range(4)]
    at, core = lax.axis_index("inner"), lax.axis_index("outer")
    y, z = at & 1, at >> 1
    odd, high, upper = (z & 1) == 1, z >= 2, y == 1
    logs = gathered_logs(last, y_pairs, z_pairs, far_pairs)
    mine = jnp.where(core == 0, logs[0], logs[1])
    index = jnp.arange(size)
    chip = index // 2

    def decay(mask):
        return jnp.exp(jnp.sum(jnp.where(mask[:, None], mine, 0.0), axis=0))

    pair_top = (z & 2) + 1
    weights = jnp.stack(
        [
            decay(index == 2 * z + 1),
            decay(chip == pair_top),
            jnp.where(high, decay((chip >= 2) & (chip < z)), 0.0),
            decay((chip >= 2) & jnp.logical_not(high)),
            decay((chip >= 2) & high),
            jnp.where(core == 1, decay(chip < z), 0.0),
            decay(index == 2 * z),
        ]
    )
    weights = jnp.repeat(weights, P_SIZE, axis=1).reshape(7, G, 1, COLS)
    entered = []
    first = 0
    for keep, send in zip(kept, sent):
        count = keep.shape[0]
        w = weights[:, first : first + count]
        got = swap(send, "inner", y_pairs).astype(F32)
        own = keep.astype(F32)
        below = jnp.where(upper, got, own)
        above = jnp.where(upper, own, got)
        chip_state = (below * w[0] + above).astype(BF16)
        got = swap(chip_state, "inner", z_pairs)
        low_chip = jnp.where(odd, got, chip_state).astype(F32)
        high_chip = jnp.where(odd, chip_state, got).astype(F32)
        two_chips = (low_chip * w[1] + high_chip).astype(BF16)
        got = swap(two_chips, "inner", mid_pairs)
        further = swap(got, "inner", z_pairs)
        inner_chip = odd != high
        others = jnp.where(inner_chip, got, further).astype(F32)
        ahead = others * w[2] + jnp.where(odd, low_chip, 0.0)
        total = (two_chips.astype(F32) * w[3] + others * w[4]).astype(BF16)
        before = swap(total, "outer", [(0, 1)]).astype(F32)
        entering = ahead + before * w[5]
        entering_above = entering * w[6] + below
        stay = jnp.where(upper, entering_above, entering).astype(BF16)
        leave = jnp.where(upper, entering, entering_above).astype(BF16)
        entered.append((stay, swap(leave, "inner", y_pairs)))
        first += count
    return entered


def combine(earlier, later):
    return (earlier[0] * later[0], later[0][:, None, :] * earlier[1] + later[1])


def enter_by_all_to_all(last, kept, sent):
    size = lax.axis_size("inner")
    upper = (lax.axis_index("inner") & 1) == 1
    keep, send = jnp.concatenate(kept), jnp.concatenate(sent)
    halves = [jnp.where(upper, send, keep), jnp.where(upper, keep, send)]
    wide = 2 * P_SIZE
    pairs = H // 2
    state = jnp.concatenate(halves, axis=1).reshape(G, N, pairs // G, wide)
    state = jnp.swapaxes(state, 1, 2).reshape(pairs, N, wide)
    decay = jnp.repeat(jnp.exp(last[0]), P_SIZE).reshape(pairs, wide)

    def spread(a):
        return lax.all_to_all(a[None], "inner", split_axis=1, concat_axis=0, tiled=True)

    decays, states = spread(decay), spread(state).astype(F32)
    run = (jnp.ones_like(decays[0]), jnp.zeros_like(states[0]))

    def lap(run, item):
        return combine(run, item), run

    total, before = lax.scan(lap, run, (decays, states))
    first = lax.ppermute(total[1].astype(BF16), "outer", [(0, 1)]).astype(F32)
    entering = before[0][:, :, None, :] * first[None] + before[1]
    carry = lax.all_to_all(
        entering.astype(BF16), "inner", split_axis=0, concat_axis=1, tiled=True
    )[0]
    carry = carry.reshape(G, pairs // G, N, wide)
    carry = jnp.swapaxes(carry, 1, 2).reshape(G, N, COLS)
    top, bottom = carry[:, :HALF], carry[:, HALF:]
    stay, got = jnp.where(upper, bottom, top), jnp.where(upper, top, bottom)
    entered = []
    at = 0
    for keep in kept:
        count = keep.shape[0]
        entered.append((stay[at : at + count], got[at : at + count]))
        at += count
    return entered


def shards(x_stream, b_stream, c_stream, dt_input, decay_log, skip_weight, conv_weight):
    tokens = x_stream.shape[0]
    rim_rows = jnp.concatenate(
        [a[tokens - RIM :] for a in (x_stream, b_stream, c_stream)], axis=1
    )
    devices = lax.axis_size("outer") * lax.axis_size("inner")
    rim = lax.ppermute(
        rim_rows, ("outer", "inner"), [(i, i + 1) for i in range(devices - 1)]
    )
    cols, rows, to_end, from_start, last = time_steps(dt_input, decay_log)
    heads = jnp.arange(2 * HEADS)[:, None] % HEADS
    spread = (jnp.arange(COLS)[None, :] // P_SIZE == heads).astype(BF16)
    skip = jnp.repeat(skip_weight, P_SIZE)[None, :]
    side = (lax.axis_index("inner") & 1).astype(jnp.int32).reshape(1)
    local = []
    first = 0
    for count in CHUNKS:
        local.append(
            end_states(
                first,
                count,
                side,
                x_stream,
                b_stream,
                c_stream,
                rim,
                conv_weight,
                to_end,
                spread,
            )
        )
        first += count
    by_swaps = lax.axis_size("inner") == 8 and lax.axis_size("outer") == 2
    enter = enter_by_swaps if by_swaps else enter_by_all_to_all
    entered = enter(last, [a[3] for a in local], [a[4] for a in local])
    out = None
    first = 0
    for count, (values, conv_b, conv_c, _, _), (keep, got) in zip(CHUNKS, local, entered):
        part = inside_block(first, count, values, conv_b, conv_c, cols, rows, skip)
        out = with_carry(
            first, count, side, conv_c, part, keep, got, from_start, spread, out
        )
        first += count
    return out


def solution(mesh):
    return jax.shard_map(
        shards,
        mesh=mesh,
        in_specs=(
            P(("slab", "outer", "inner"), None),
            P(("slab", "outer", "inner"), None),
            P(("slab", "outer", "inner"), None),
            P(("slab", "outer", "inner"), None),
            P("slab"),
            P(),
            P(),
        ),
        out_specs=P(("slab", "outer", "inner"), None),
        check_vma=False,
    )
```

```python
import jax
import jax.numpy as jnp
from jax import lax
from jax.experimental import pallas as pl
from jax.experimental.pallas import tpu as pltpu
from jax.sharding import PartitionSpec as P

H = 128
P_SIZE = 64
N = 128
G = 8
KERNEL_TAPS = 4
SPAN = 256

HEADS = H // G
COLS = HEADS * P_SIZE
HALF = N // 2
RIM = KERNEL_TAPS - 1
PAD = 8
LOG2E = 1.4426950408889634
VMEM = 16 * 1024 * 1024
TILE = 16
WIDE = H * P_SIZE
F32 = jnp.float32
BF16 = jnp.bfloat16
CHUNKS = (2, 2, 2, 2)


def params():
    return pltpu.CompilerParams(vmem_limit_bytes=VMEM)


def cost(us, moved=0):
    return pl.CostEstimate(flops=int(us * 9e8), bytes_accessed=moved, transcendentals=0)


def mark():
    return jax.ShapeDtypeStruct((8, 128), F32)


MARK = pl.BlockSpec((8, 128), lambda i: (0, 0))


def corner(a):
    tile = tuple(min(n, m) for n, m in zip(a.shape[-2:], (TILE, 128)))
    block = (1,) * (a.ndim - 2) + tile
    return pl.BlockSpec(block, lambda i: (0,) * a.ndim)


def rim_body(x_ref, b_ref, c_ref, rim_ref):
    rim_ref[:, :WIDE] = x_ref[TILE - RIM :, :]
    rim_ref[:, WIDE : WIDE + G * N] = b_ref[TILE - RIM :, :]
    rim_ref[:, WIDE + G * N :] = c_ref[TILE - RIM :, :]


def rim_rows(x, b, c):
    at = x.shape[0] // TILE - 1
    width = x.shape[1] + b.shape[1] + c.shape[1]
    return pl.pallas_call(
        rim_body,
        grid=(1,),
        in_specs=[pl.BlockSpec((TILE, a.shape[1]), lambda i: (at, 0)) for a in (x, b, c)],
        out_specs=pl.BlockSpec((RIM, width), lambda i: (0, 0)),
        out_shape=jax.ShapeDtypeStruct((RIM, width), BF16),
        compiler_params=params(),
        cost_estimate=cost(1.0),
        name="rim_rows",
    )(*[pltpu.with_memory_space_constraint(a, pltpu.HBM) for a in (x, b, c)])


def whole(a):
    return pl.BlockSpec(a.shape, lambda i: (0,) * len(a.shape))


def split(value, parts):
    found = []
    for _ in range(parts):
        found.append(value.astype(BF16))
        value = value - found[-1].astype(F32)
    groups = []
    for group in range(G):
        lo = group * HEADS
        groups.append(jnp.concatenate([a[:, lo : lo + HEADS] for a in found], axis=1))
    return groups


def spreader(parts):
    head = lax.broadcasted_iota(jnp.int32, (parts * HEADS, COLS), 0) % HEADS
    col = lax.broadcasted_iota(jnp.int32, (parts * HEADS, COLS), 1) // P_SIZE
    return jnp.where(head == col, 1.0, 0.0).astype(BF16)


def by_column(value, matrix, parts):
    rows = jnp.concatenate(split(value, parts), axis=0)
    return jnp.dot(rows, matrix, preferred_element_type=F32)


def steps_body(
    dt_ref,
    decay_ref,
    skip_ref,
    cols_ref,
    rows_ref,
    to_end_ref,
    from_start_ref,
    last_ref,
    skip_cols_ref,
    spread_ref,
):
    raw = dt_ref[...].astype(F32)
    dt = jnp.maximum(raw, 0.0) + jnp.log1p(jnp.exp(-jnp.abs(raw)))
    step = dt * (-jnp.exp(decay_ref[...]))
    row = lax.broadcasted_iota(jnp.int32, (SPAN, SPAN), 0)
    col = lax.broadcasted_iota(jnp.int32, (SPAN, SPAN), 1)
    tri = jnp.where(row >= col, 1.0, 0.0).astype(F32)
    cum = jnp.dot(tri, step, precision=lax.Precision.HIGHEST, preferred_element_type=F32)
    last = cum[SPAN - 1 :, :]
    last_ref[...] = last
    rows_ref[...] = jnp.transpose((cum - jnp.log(dt)) * LOG2E)
    to_end = split(jnp.exp(last - cum) * dt, 2)
    from_start = split(jnp.exp(cum), 2)
    scaled = cum * LOG2E
    for group in range(G):
        lo = group * HEADS
        cols_ref[group] = scaled[:, lo : lo + HEADS]
        to_end_ref[group] = to_end[group]
        from_start_ref[group] = from_start[group]
    skip_cols = by_column(skip_ref[...], spreader(3), 3)
    for group in range(G):
        skip_cols_ref[group] = skip_cols[group : group + 1]
    spread_ref[...] = spreader(2)


def time_steps(dt_input, decay_log, skip_weight):
    given = (dt_input, decay_log.reshape(1, H), skip_weight.reshape(1, H))
    out = [
        jax.ShapeDtypeStruct((G, SPAN, HEADS), F32),
        jax.ShapeDtypeStruct((H, SPAN), F32),
        jax.ShapeDtypeStruct((G, SPAN, 2 * HEADS), BF16),
        jax.ShapeDtypeStruct((G, SPAN, 2 * HEADS), BF16),
        jax.ShapeDtypeStruct((1, H), F32),
        jax.ShapeDtypeStruct((G, 1, COLS), F32),
        jax.ShapeDtypeStruct((2 * HEADS, COLS), BF16),
    ]
    return pl.pallas_call(
        steps_body,
        grid=(1,),
        in_specs=[whole(a) for a in given],
        out_specs=[whole(a) for a in out],
        out_shape=out,
        compiler_params=params(),
        cost_estimate=cost(2.0),
        name="time_steps",
    )(*given)


def convolved(ref, rim_ref, kernel_ref, scratch):
    kernel = kernel_ref[...].astype(F32) * 0.5
    width = ref.shape[1]
    parts = []
    for lo in range(0, width, 128):
        sl = slice(lo, lo + 128)
        scratch[PAD - RIM : PAD, :] = rim_ref[:, sl].astype(F32)
        scratch[PAD : PAD + SPAN, :] = ref[:, sl].astype(F32)
        half = kernel[RIM : RIM + 1, sl] * scratch[PAD : PAD + SPAN, :]
        for tap in range(RIM):
            first = PAD - RIM + tap
            half = half + kernel[tap : tap + 1, sl] * scratch[first : first + SPAN, :]
        parts.append((half + half * jnp.tanh(half)).astype(BF16))
    return parts


def states_body(
    x_ref,
    b_ref,
    c_ref,
    rim_x_ref,
    rim_b_ref,
    rim_c_ref,
    kernel_x_ref,
    kernel_b_ref,
    kernel_c_ref,
    to_end_ref,
    spread_ref,
    flag_ref,
    last_ref,
    values_ref,
    conv_b_ref,
    conv_c_ref,
    keep_ref,
    send_ref,
    mark_ref,
    scratch,
):
    mark_ref[...] = jnp.zeros_like(mark_ref)
    (conv_b,) = convolved(b_ref, rim_b_ref, kernel_b_ref, scratch)
    (conv_c,) = convolved(c_ref, rim_c_ref, kernel_c_ref, scratch)
    conv_b_ref[...] = conv_b
    conv_c_ref[...] = conv_c
    parts = convolved(x_ref, rim_x_ref, kernel_x_ref, scratch)
    for at, part in enumerate(parts):
        values_ref[:, at * 128 : (at + 1) * 128] = part
    gain = jnp.dot(to_end_ref[0], spread_ref[...], preferred_element_type=F32)
    weighted = (values_ref[...].astype(F32) * gain).astype(BF16)
    state = lax.dot_general(
        conv_b, weighted, (((0,), (0,)), ((), ())), preferred_element_type=F32
    ).astype(BF16)
    upper = flag_ref[:1] > 0.5
    at = pl.program_id(0)
    rows = pl.ds(pl.multiple_of(at * HALF, HALF), HALF)
    keep_ref[rows, :] = jnp.where(upper, state[HALF:], state[:HALF])
    send_ref[rows, :] = jnp.where(upper, state[:HALF], state[HALF:])
    if send_ref.shape[0] > keep_ref.shape[0]:
        put_log(send_ref, keep_ref.shape[0], last_ref[...])


def end_states(first, count, x, b, c, rim, conv_weight, to_end, spread, flags, last, after, us=1.0):
    def cols(offset):
        return lambda i: (0, offset + first + i)

    def own(i):
        return (0, i)

    def lead(i):
        return (first + i, 0, 0)

    b_at, c_at = H * P_SIZE // N, H * P_SIZE // N + G
    return pl.pallas_call(
        lambda *refs: states_body(*refs[:13], *refs[13 + len(after) :]),
        grid=(count,),
        in_specs=[
            pl.BlockSpec((SPAN, COLS), cols(0)),
            pl.BlockSpec((SPAN, N), cols(0)),
            pl.BlockSpec((SPAN, N), cols(0)),
            pl.BlockSpec((RIM, COLS), cols(0)),
            pl.BlockSpec((RIM, N), cols(b_at)),
            pl.BlockSpec((RIM, N), cols(c_at)),
            pl.BlockSpec((KERNEL_TAPS, COLS), cols(0)),
            pl.BlockSpec((KERNEL_TAPS, N), cols(b_at)),
            pl.BlockSpec((KERNEL_TAPS, N), cols(c_at)),
            pl.BlockSpec((1, SPAN, 2 * HEADS), lead),
            pl.BlockSpec((2 * HEADS, COLS), lambda i: (0, 0)),
            whole(flags),
            whole(last),
        ]
        + [corner(a) for a in after],
        out_specs=[
            pl.BlockSpec((SPAN, COLS), own),
            pl.BlockSpec((SPAN, N), own),
            pl.BlockSpec((SPAN, N), own),
            pl.BlockSpec((count * HALF, COLS), lambda i: (0, 0)),
            pl.BlockSpec((count * HALF + log_rows(first), COLS), lambda i: (0, 0)),
            MARK,
        ],
        out_shape=[
            jax.ShapeDtypeStruct((SPAN, count * COLS), BF16),
            jax.ShapeDtypeStruct((SPAN, count * N), BF16),
            jax.ShapeDtypeStruct((SPAN, count * N), BF16),
            jax.ShapeDtypeStruct((count * HALF, COLS), BF16),
            jax.ShapeDtypeStruct((count * HALF + log_rows(first), COLS), BF16),
            mark(),
        ],
        scratch_shapes=[pltpu.VMEM((PAD + SPAN, 128), F32)],
        compiler_params=params(),
        cost_estimate=cost(us),
        name="end_states",
    )(x, b, c, rim, rim, rim, conv_weight, conv_weight, conv_weight, to_end, spread, flags, last, *after)


def inside_body(values_ref, b_ref, c_ref, cols_ref, rows_ref, skip_ref, part_ref, mark_ref):
    mark_ref[...] = jnp.zeros_like(mark_ref)
    half = SPAN // 2
    scores = lax.dot_general(
        c_ref[...], b_ref[...], (((1,), (1,)), ((), ())), preferred_element_type=F32
    )
    row = lax.broadcasted_iota(jnp.int32, (half, half), 0)
    col = lax.broadcasted_iota(jnp.int32, (half, half), 1)
    causal = row >= col
    lane = lax.broadcasted_iota(jnp.int32, (half, 2 * P_SIZE), 1)
    first_head = lane < P_SIZE
    cols = cols_ref[0]
    rows = rows_ref[...]
    corner, below, later = scores[:half, :half], scores[half:, :half], scores[half:, half:]
    for pair in range(HEADS // 2):
        upper, lower = [], []
        for head in (2 * pair, 2 * pair + 1):
            at_t = cols[:, head : head + 1]
            at_s = rows[head : head + 1, :]
            e = jnp.exp2(at_t[:half] - at_s[:, :half])
            upper.append(jnp.where(causal, corner * e, 0.0).astype(BF16))
            e = jnp.exp2(at_t[half:] - at_s[:, :half])
            left = (below * e).astype(BF16)
            e = jnp.exp2(at_t[half:] - at_s[:, half:])
            right = jnp.where(causal, later * e, 0.0).astype(BF16)
            lower.append(jnp.concatenate([left, right], axis=1))
        sl = slice(pair * 2 * P_SIZE, (pair + 1) * 2 * P_SIZE)
        values = values_ref[:, sl]
        skip = skip_ref[0, :, sl]
        for lo, mix, depth in ((0, upper, half), (half, lower, SPAN)):
            both = jnp.dot(
                jnp.concatenate(mix, axis=0), values[:depth], preferred_element_type=F32
            )
            inside = jnp.where(first_head, both[:half], both[half:])
            part_ref[lo : lo + half, sl] = inside + skip * values[lo : lo + half].astype(F32)


def inside_block(first, count, values, conv_b, conv_c, cols, rows, skip, after, us=1.0):
    def own(i):
        return (0, i)

    return pl.pallas_call(
        lambda *refs: inside_body(*refs[:6], *refs[6 + len(after) :]),
        grid=(count,),
        in_specs=[
            pl.BlockSpec((SPAN, COLS), own),
            pl.BlockSpec((SPAN, N), own),
            pl.BlockSpec((SPAN, N), own),
            pl.BlockSpec((1, SPAN, HEADS), lambda i: (first + i, 0, 0)),
            pl.BlockSpec((HEADS, SPAN), lambda i: (first + i, 0)),
            pl.BlockSpec((1, 1, COLS), lambda i: (first + i, 0, 0)),
        ]
        + [corner(a) for a in after],
        out_specs=[pl.BlockSpec((SPAN, COLS), own), MARK],
        out_shape=[jax.ShapeDtypeStruct((SPAN, count * COLS), F32), mark()],
        compiler_params=params(),
        cost_estimate=cost(us),
        name="inside_block",
    )(values, conv_b, conv_c, cols, rows, skip, *after)


def carried_body(*refs):
    side_ref, c_ref, part_ref, keep_ref, got_ref, from_start_ref, spread_ref = refs[:7]
    out_ref, mark_ref = refs[-2:]
    mark_ref[...] = jnp.zeros_like(mark_ref)
    upper = side_ref[:1] > 0.5
    keep, got = keep_ref[...], got_ref[...]
    carry = jnp.concatenate(
        [jnp.where(upper, got, keep), jnp.where(upper, keep, got)], axis=0
    )
    gain = jnp.dot(from_start_ref[0], spread_ref[...], preferred_element_type=F32)
    carried = jnp.dot(c_ref[...], carry, preferred_element_type=F32)
    out_ref[...] = (part_ref[...] + carried * gain).astype(BF16)


def with_carry(first, count, side, conv_c, part, keep, got, from_start, spread, out, after, us=1.0):
    def own(i):
        return (0, i)

    given = [] if out is None else [out]
    return pl.pallas_call(
        carried_body,
        grid=(count,),
        in_specs=[
            whole(side),
            pl.BlockSpec((SPAN, N), own),
            pl.BlockSpec((SPAN, COLS), own),
            pl.BlockSpec((HALF, COLS), lambda i: (i, 0)),
            pl.BlockSpec((HALF, COLS), lambda i: (i, 0)),
            pl.BlockSpec((1, SPAN, 2 * HEADS), lambda i: (first + i, 0, 0)),
            pl.BlockSpec((2 * HEADS, COLS), lambda i: (0, 0)),
        ]
        + [pl.BlockSpec(memory_space=pl.ANY)] * len(given)
        + [corner(a) for a in after],
        out_specs=[pl.BlockSpec((SPAN, COLS), lambda i: (0, first + i)), MARK],
        out_shape=[jax.ShapeDtypeStruct((SPAN, WIDE), BF16), mark()],
        input_output_aliases={7: 0} if given else {},
        compiler_params=params(),
        cost_estimate=cost(us),
        name="with_carry",
    )(side, conv_c, part, keep, got, from_start, spread, *given, *after)


def swap(value, axis, pairs):
    return lax.ppermute(value, axis, pairs + [(b, a) for a, b in pairs])


def log_rows(first):
    return TILE if first == 0 else 0


def put_log(ref, at, log):
    ref[at:, :] = jnp.zeros((TILE, COLS), BF16)
    parts = []
    for _ in range(3):
        parts.append(log.astype(BF16).astype(F32))
        log = log - parts[-1]
    rest = jnp.zeros((TILE - len(parts), H), F32)
    ref[at:, :H] = jnp.concatenate(parts + [rest], axis=0).astype(BF16)


def take_log(ref, at):
    rows = ref[at:, :H].astype(F32)
    return rows[0:1] + rows[1:2] + rows[2:3]


Y_PAIRS = [(0, 1), (2, 3), (4, 5), (6, 7)]
Z_PAIRS = [(0, 2), (1, 3), (4, 6), (5, 7)]
MID_PAIRS = [(2, 4), (3, 5)]
FAR_PAIRS = [(0, 4), (1, 5), (2, 6), (3, 7)]

ORDER = (
    [("state", 0, 1.0), ("state", 1, 1.0), ("state", 2, 1.0), ("chip", 0, 1.0)]
    + [("state", 3, 1.0), ("chip", 1, 1.0), ("chips", 0, 1.0), ("chip", 2, 1.0)]
    + [("chips", 1, 1.0), ("link", 0, 1.0), ("chips", 2, 1.0), ("chip", 3, 1.0)]
    + [("inside", 3, 1.0), ("link", 1, 1.0), ("total", 0, 1.0), ("link", 2, 1.0)]
    + [("inside", 0, 1.0), ("chips", 3, 1.0), ("inside", 1, 1.0), ("leave", 0, 1.0)]
    + [("total", 1, 1.0), ("link", 3, 1.0), ("total", 2, 1.0), ("leave", 1, 1.0)]
    + [("out", 0, 1.0), ("total", 3, 1.0), ("leave", 2, 1.0), ("inside", 2, 1.0)]
    + [("out", 1, 1.0), ("leave", 3, 1.0), ("out", 2, 1.0), ("out", 3, 1.0)]
)


def places():
    at, core = lax.axis_index("inner"), lax.axis_index("outer")
    z = at >> 1
    row = lax.broadcasted_iota(jnp.int32, (8, COLS), 0)
    flags = jnp.zeros((8, COLS), F32)
    for number, flag in enumerate(((at & 1) == 1, (z & 1) == 1, z >= 2, core == 1)):
        flags = jnp.where((row == number) & flag, 1.0, flags)
    return flags


def merge(body, arrays, weights, lead, flags, spread, after, outs, us):
    count = min(a.shape[0] for a in arrays) // HALF
    rows = count * HALF
    given = [flags, *arrays]
    out = [jax.ShapeDtypeStruct((rows, COLS), BF16)] * outs
    given += weights
    if lead is not None:
        step, known, wanted, sends = lead
        given += [spread, known]
        if sends:
            out = [jax.ShapeDtypeStruct((rows + TILE, COLS), BF16)]
        out.append(jax.ShapeDtypeStruct((8, H), F32))
        out += [jax.ShapeDtypeStruct((n, 1, COLS), F32) for n in CHUNKS] * wanted
    out.append(mark())

    def run(*refs):
        ins = refs[1 : 1 + len(arrays)]
        scale_refs = refs[1 + len(arrays) : 1 + len(arrays) + len(weights)]
        rest = refs[1 + len(arrays) + len(weights) : len(given)]
        results = refs[len(given) + len(after) :]
        on = [refs[0][at : at + 1] > 0.5 for at in range(4)]
        results[-1][...] = jnp.zeros((8, 128), F32)
        scales = [[r[at] for r in scale_refs] for at in range(count)]
        if lead is not None:
            logs = [take_log(r, rows) if r.shape[0] > rows else None for r in ins]
            found, keeps, onward = step([a[:, :H] for a in on], logs, rest[1][...])
            empty = jnp.zeros((8 - len(keeps), H), F32)
            results[outs][...] = jnp.concatenate(keeps + [empty], axis=0)
            if sends:
                put_log(results[0], rows, onward)
            found = [by_column(row, rest[0][...], 2) for row in found]
            scales = [[f[at : at + 1] for f in found] + scales[at] for at in range(count)]
            at = outs + 1
            for value in found:
                first = 0
                for n in CHUNKS:
                    for group in range(n):
                        results[at][group] = value[first + group : first + group + 1]
                    first += n
                    at += 1
        for at in range(count):
            part = slice(at * HALF, (at + 1) * HALF)
            values = body(on, [r[part, :].astype(F32) for r in ins], scales[at])
            for ref, value in zip(results, values):
                ref[part, :] = value.astype(BF16)

    found = pl.pallas_call(
        run,
        grid=(1,),
        in_specs=[whole(a) for a in given] + [corner(a) for a in after],
        out_specs=[whole(a) for a in out],
        out_shape=out,
        compiler_params=params(),
        cost_estimate=cost(us),
        name=body.__name__,
    )(*given, *after)
    if lead is None:
        return found[:outs], found[-1], None, None
    n = len(CHUNKS)
    scales = [found[outs + 1 + n * at : outs + 1 + n * (at + 1)] for at in range(wanted)]
    return found[:outs], found[-1], found[outs], scales


def add_chip(on, arrays, scales):
    upper, _, _, _ = on
    keep, got = arrays
    return (jnp.where(upper, got, keep) * scales[0] + jnp.where(upper, keep, got),)


def chip_logs(on, logs, known):
    upper, _, _, _ = on
    own, got = known[0:1], logs[1]
    low, high = jnp.where(upper, got, own), jnp.where(upper, own, got)
    return [jnp.exp(high), jnp.exp(low)], [low + high], low + high


def add_chips(on, arrays, scales):
    _, odd, _, _ = on
    chip, got = arrays
    return (jnp.where(odd, got, chip) * scales[0] + jnp.where(odd, chip, got),)


def chips_logs(on, logs, known):
    _, odd, _, _ = on
    own, got = known[0:1], logs[1]
    low, high = jnp.where(odd, got, own), jnp.where(odd, own, got)
    return [jnp.exp(high), jnp.exp(own)], [low + high, low], low + high


def go_on(on, arrays, scales):
    _, _, high, _ = on
    chip, two, got = arrays
    own, other, through = scales
    return (jnp.where(high, got * through + chip, two * own + got * other),)


def go_on_logs(on, logs, known):
    _, _, high, _ = on
    own, low, got = known[0:1], known[1:2], logs[2]
    none = jnp.zeros_like(own)
    weights = [jnp.exp(jnp.where(high, none, got)), jnp.exp(jnp.where(high, own, none))]
    return weights, [got, low], got


def add_all(on, arrays, scales):
    _, odd, high, _ = on
    chip, two, got, far = arrays
    own, other, through = scales[:3]
    at_end = jnp.where(high, far * through + chip, far)
    return (jnp.where(odd != high, two * own + got * other, at_end),)


def enter_logs(on, logs, known):
    _, odd, high, core = on
    other, low, further = known[0:1], known[1:2], logs[4]
    none = jnp.zeros_like(other)
    below = jnp.where(odd, low, none)
    reach = jnp.where(high, jnp.where(odd, further, other), none) + below
    return [jnp.where(core, jnp.exp(reach), none)], [], None


def enter(on, arrays, scales):
    upper, odd, high, _ = on
    keep, got_y, got_z, got, far, before = arrays
    reach, below = scales
    low_side = jnp.where(odd, got_z, jnp.zeros_like(got_z))
    entering = jnp.where(high, jnp.where(odd, far, got), low_side) + before * reach
    above = entering * below + jnp.where(upper, got_y, keep)
    return jnp.where(upper, above, entering), jnp.where(upper, entering, above)


def in_order(x, b, c, rim, conv_weight, steps, flags):
    cols, rows, to_end, from_start, last, skip, spread = steps
    starts = [sum(CHUNKS[:k]) for k in range(len(CHUNKS))]
    done, weights = {}, {}
    known = last
    after = []
    out = None

    def merged(body, k, names, scales, logs, wanted, outs=1, sends=True):
        nonlocal known
        lead = (logs, known, len(wanted), sends) if k == 0 and logs is not None else None
        if lead is None:
            scales = wanted + scales
        found, mark, keeps, new = merge(
            body,
            [done[name, k] for name in names],
            [weights[name][k] for name in scales],
            lead,
            flags,
            spread,
            after,
            outs,
            us,
        )
        if lead is not None:
            known = keeps
            weights.update(zip(wanted, new))
        return found, mark

    for what, k, us in ORDER:
        first, count = starts[k], CHUNKS[k]
        if what == "state":
            found = end_states(
                first, count, x, b, c, rim, conv_weight, to_end, spread, flags, last, after, us
            )
            done["values", k], done["b", k], done["c", k], keep, send, mark = found
            done["keep", k], done["y", k] = keep, swap(send, "inner", Y_PAIRS)
        elif what == "inside":
            given = [done[name, k] for name in ("values", "b", "c")]
            done["inside", k], mark = inside_block(
                first, count, *given, cols, rows, skip, after, us
            )
        elif what == "chip":
            wanted = ["above", "below"]
            if k > 0:
                wanted = ["above"]
            (found,), mark = merged(add_chip, k, ["keep", "y"], [], chip_logs, wanted)
            done["chip", k], done["z", k] = found, swap(found, "inner", Z_PAIRS)
        elif what == "chips":
            wanted = ["high", "through"]
            if k > 0:
                wanted = ["high"]
            (found,), mark = merged(add_chips, k, ["chip", "z"], [], chips_logs, wanted)
            done["chips", k], done["mid", k] = found, swap(found, "inner", MID_PAIRS)
        elif what == "link":
            names = ["chip", "chips", "mid"]
            (found,), mark = merged(
                go_on, k, names, ["through"], go_on_logs, ["own", "other"]
            )
            done["far", k] = swap(found, "inner", Z_PAIRS)
        elif what == "total":
            names = ["chip", "chips", "mid", "far"]
            (found,), mark = merged(
                add_all, k, names, ["own", "other", "through"], None, []
            )
            done["before", k] = swap(found, "outer", [(0, 1)])
        elif what == "leave":
            names = ["keep", "y", "z", "mid", "far", "before"]
            (stay, leave), mark = merged(
                enter, k, names, ["below"], enter_logs, ["reach"], outs=2, sends=False
            )
            done["stay", k], done["back", k] = stay, swap(leave, "inner", Y_PAIRS)
        else:
            given = [done[name, k] for name in ("c", "inside", "stay", "back")]
            out, mark = with_carry(
                first, count, flags, *given, from_start, spread, out, after, us
            )
        after = [mark]
    return out


def combine(earlier, later):
    return (earlier[0] * later[0], later[0][:, None, :] * earlier[1] + later[1])


def enter_by_all_to_all(last, kept, sent):
    size = lax.axis_size("inner")
    upper = (lax.axis_index("inner") & 1) == 1
    wide = 2 * P_SIZE
    pairs = H // 2
    sent = [a[: b.shape[0]] for a, b in zip(sent, kept)]
    keep, send = [jnp.concatenate(a).reshape(G, HALF, COLS) for a in (kept, sent)]
    halves = [jnp.where(upper, send, keep), jnp.where(upper, keep, send)]
    state = jnp.concatenate(halves, axis=1).reshape(G, N, pairs // G, wide)
    state = jnp.swapaxes(state, 1, 2).reshape(pairs, N, wide)
    decay = jnp.repeat(jnp.exp(last[0]), P_SIZE).reshape(pairs, wide)

    def spread(a):
        return lax.all_to_all(a[None], "inner", split_axis=1, concat_axis=0, tiled=True)

    decays, states = spread(decay), spread(state).astype(F32)
    run = (jnp.ones_like(decays[0]), jnp.zeros_like(states[0]))

    def lap(run, item):
        return combine(run, item), run

    total, before = lax.scan(lap, run, (decays, states))
    first = lax.ppermute(total[1].astype(BF16), "outer", [(0, 1)]).astype(F32)
    entering = before[0][:, :, None, :] * first[None] + before[1]
    carry = lax.all_to_all(
        entering.astype(BF16), "inner", split_axis=0, concat_axis=1, tiled=True
    )[0]
    carry = carry.reshape(G, pairs // G, N, wide)
    carry = jnp.swapaxes(carry, 1, 2).reshape(G, N, COLS)
    top, bottom = carry[:, :HALF], carry[:, HALF:]
    stay, got = jnp.where(upper, bottom, top), jnp.where(upper, top, bottom)
    entered = []
    at = 0
    for count in CHUNKS:
        part = [a[at : at + count].reshape(count * HALF, COLS) for a in (stay, got)]
        entered.append(part)
        at += count
    return entered


def one_by_one(x, b, c, rim, conv_weight, steps, flags):
    cols, rows, to_end, from_start, last, skip, spread = steps
    starts = [sum(CHUNKS[:k]) for k in range(len(CHUNKS))]
    states = [
        end_states(
            first, count, x, b, c, rim, conv_weight, to_end, spread, flags, last, []
        )
        for first, count in zip(starts, CHUNKS)
    ]
    entered = enter_by_all_to_all(last, [a[3] for a in states], [a[4] for a in states])
    out = None
    for first, count, state, (keep, got) in zip(starts, CHUNKS, states, entered):
        values, conv_b, conv_c = state[:3]
        part, _ = inside_block(
            first, count, values, conv_b, conv_c, cols, rows, skip, []
        )
        out, _ = with_carry(
            first, count, flags, conv_c, part, keep, got, from_start, spread, out, []
        )
    return out


def shards(x_stream, b_stream, c_stream, dt_input, decay_log, skip_weight, conv_weight):
    devices = lax.axis_size("outer") * lax.axis_size("inner")
    x_stream, dt_input, flags = lax.optimization_barrier((x_stream, dt_input, places()))
    rim = lax.ppermute(
        rim_rows(x_stream, b_stream, c_stream),
        ("outer", "inner"),
        [(i, i + 1) for i in range(devices - 1)],
    )
    steps = time_steps(dt_input, decay_log, skip_weight)
    by_swaps = lax.axis_size("inner") == 8 and lax.axis_size("outer") == 2
    rest = in_order if by_swaps else one_by_one
    return rest(x_stream, b_stream, c_stream, rim, conv_weight, steps, flags)


def solution(mesh):
    return jax.shard_map(
        shards,
        mesh=mesh,
        in_specs=(
            P(("slab", "outer", "inner"), None),
            P(("slab", "outer", "inner"), None),
            P(("slab", "outer", "inner"), None),
            P(("slab", "outer", "inner"), None),
            P("slab"),
            P(),
            P(),
        ),
        out_specs=P(("slab", "outer", "inner"), None),
        check_vma=False,
    )
```

```python
import jax
import jax.numpy as jnp
from jax import lax
from jax.experimental import pallas as pl
from jax.experimental.pallas import tpu as pltpu
from jax.sharding import PartitionSpec as P

H = 128
P_SIZE = 64
N = 128
G = 8
KERNEL_TAPS = 4
SPAN = 256

HEADS = H // G
COLS = HEADS * P_SIZE
HALF = N // 2
RIM = KERNEL_TAPS - 1
PAD = 8
LOG2E = 1.4426950408889634
VMEM = 16 * 1024 * 1024
TILE = 16
WIDE = H * P_SIZE
F32 = jnp.float32
BF16 = jnp.bfloat16
CHUNKS = (2, 2, 2, 2)


def params():
    return pltpu.CompilerParams(vmem_limit_bytes=VMEM)


def cost(us, moved=0):
    return pl.CostEstimate(flops=int(us * 6e8), bytes_accessed=moved, transcendentals=0)


def mark():
    return jax.ShapeDtypeStruct((8, 128), F32)


MARK = pl.BlockSpec((8, 128), lambda i: (0, 0))


def corner(a):
    tile = tuple(min(n, m) for n, m in zip(a.shape[-2:], (TILE, 128)))
    block = (1,) * (a.ndim - 2) + tile
    return pl.BlockSpec(block, lambda i: (0,) * a.ndim)


def rim_body(x_ref, b_ref, c_ref, rim_ref):
    rim_ref[:, :WIDE] = x_ref[TILE - RIM :, :]
    rim_ref[:, WIDE : WIDE + G * N] = b_ref[TILE - RIM :, :]
    rim_ref[:, WIDE + G * N :] = c_ref[TILE - RIM :, :]


def rim_rows(x, b, c):
    at = x.shape[0] // TILE - 1
    width = x.shape[1] + b.shape[1] + c.shape[1]
    return pl.pallas_call(
        rim_body,
        grid=(1,),
        in_specs=[pl.BlockSpec((TILE, a.shape[1]), lambda i: (at, 0)) for a in (x, b, c)],
        out_specs=pl.BlockSpec((RIM, width), lambda i: (0, 0)),
        out_shape=jax.ShapeDtypeStruct((RIM, width), BF16),
        compiler_params=params(),
        cost_estimate=cost(1.0),
        name="rim_rows",
    )(*[pltpu.with_memory_space_constraint(a, pltpu.HBM) for a in (x, b, c)])


def whole(a):
    return pl.BlockSpec(a.shape, lambda i: (0,) * len(a.shape))


def split(value, parts):
    found = []
    for _ in range(parts):
        found.append(value.astype(BF16))
        value = value - found[-1].astype(F32)
    groups = []
    for group in range(G):
        lo = group * HEADS
        groups.append(jnp.concatenate([a[:, lo : lo + HEADS] for a in found], axis=1))
    return groups


def spreader(parts):
    head = lax.broadcasted_iota(jnp.int32, (parts * HEADS, COLS), 0) % HEADS
    col = lax.broadcasted_iota(jnp.int32, (parts * HEADS, COLS), 1) // P_SIZE
    return jnp.where(head == col, 1.0, 0.0).astype(BF16)


def by_column(value, matrix, parts):
    rows = jnp.concatenate(split(value, parts), axis=0)
    return jnp.dot(rows, matrix, preferred_element_type=F32)


def steps_body(
    dt_ref,
    decay_ref,
    skip_ref,
    cols_ref,
    rows_ref,
    to_end_ref,
    from_start_ref,
    last_ref,
    skip_cols_ref,
    spread_ref,
):
    raw = dt_ref[...].astype(F32)
    dt = jnp.maximum(raw, 0.0) + jnp.log1p(jnp.exp(-jnp.abs(raw)))
    step = dt * (-jnp.exp(decay_ref[...]))
    row = lax.broadcasted_iota(jnp.int32, (SPAN, SPAN), 0)
    col = lax.broadcasted_iota(jnp.int32, (SPAN, SPAN), 1)
    tri = jnp.where(row >= col, 1.0, 0.0).astype(F32)
    cum = jnp.dot(tri, step, precision=lax.Precision.HIGHEST, preferred_element_type=F32)
    last = cum[SPAN - 1 :, :]
    last_ref[...] = last
    rows_ref[...] = jnp.transpose((cum - jnp.log(dt)) * LOG2E)
    to_end = split(jnp.exp(last - cum) * dt, 2)
    from_start = split(jnp.exp(cum), 2)
    scaled = cum * LOG2E
    for group in range(G):
        lo = group * HEADS
        cols_ref[group] = scaled[:, lo : lo + HEADS]
        to_end_ref[group] = to_end[group]
        from_start_ref[group] = from_start[group]
    skip_cols = by_column(skip_ref[...], spreader(3), 3)
    for group in range(G):
        skip_cols_ref[group] = skip_cols[group : group + 1]
    spread_ref[...] = spreader(2)


def time_steps(dt_input, decay_log, skip_weight):
    given = (dt_input, decay_log.reshape(1, H), skip_weight.reshape(1, H))
    out = [
        jax.ShapeDtypeStruct((G, SPAN, HEADS), F32),
        jax.ShapeDtypeStruct((H, SPAN), F32),
        jax.ShapeDtypeStruct((G, SPAN, 2 * HEADS), BF16),
        jax.ShapeDtypeStruct((G, SPAN, 2 * HEADS), BF16),
        jax.ShapeDtypeStruct((1, H), F32),
        jax.ShapeDtypeStruct((G, 1, COLS), F32),
        jax.ShapeDtypeStruct((2 * HEADS, COLS), BF16),
    ]
    return pl.pallas_call(
        steps_body,
        grid=(1,),
        in_specs=[whole(a) for a in given],
        out_specs=[whole(a) for a in out],
        out_shape=out,
        compiler_params=params(),
        cost_estimate=cost(2.0),
        name="time_steps",
    )(*given)


def convolved(now, rim, kernel, scratch):
    kernel = kernel.astype(F32) * 0.5
    tokens = now.shape[0]
    now = now.astype(F32)
    scratch[PAD - RIM : PAD, :] = rim.astype(F32)
    scratch[PAD : PAD + tokens, :] = now
    half = kernel[RIM : RIM + 1] * now
    for tap in range(RIM):
        first = PAD - RIM + tap
        half = half + kernel[tap : tap + 1] * scratch[first : first + tokens, :]
    return (half + half * jnp.tanh(half)).astype(BF16)


def give_state(state, at, flag_ref, last_ref, keep_ref, send_ref):
    upper = flag_ref[:1] > 0.5
    rows = pl.ds(pl.multiple_of(at * HALF, HALF), HALF)
    keep_ref[rows, :] = jnp.where(upper, state[HALF:], state[:HALF])
    send_ref[rows, :] = jnp.where(upper, state[:HALF], state[HALF:])
    if send_ref.shape[0] > keep_ref.shape[0]:
        put_log(send_ref, keep_ref.shape[0], last_ref[...])


def states_body(skipped, given, outs, scratch):
    x_ref, b_ref, c_ref, kernel_x_ref, kernel_b_ref, kernel_c_ref, to_end_ref, spread_ref = given[:8]
    values_ref, conv_b_ref, conv_c_ref = outs[:3]
    rims = given[8:11] if not skipped else [None] * 3
    tokens = x_ref.shape[0]

    def conv(ref, rim_ref, kernel_ref, lo, turn):
        sl = slice(lo, lo + 128)
        rim = jnp.zeros((RIM, 128), F32) if rim_ref is None else rim_ref[:, sl]
        return convolved(ref[:, sl], rim, kernel_ref[:, sl], scratch.at[turn])

    conv_b = conv(b_ref, rims[1], kernel_b_ref, 0, 0)
    conv_b_ref[...] = conv_b
    conv_c_ref[...] = conv(c_ref, rims[2], kernel_c_ref, 0, 1)
    gain = jnp.dot(to_end_ref[0], spread_ref[...], preferred_element_type=F32)
    weighted = []
    for at in range(x_ref.shape[1] // 128):
        sl = slice(at * 128, (at + 1) * 128)
        part = conv(x_ref, rims[0], kernel_x_ref, at * 128, at % 2)
        values_ref[:, sl] = part
        weighted.append((part.astype(F32) * gain[:, sl]).astype(BF16))
    weighted = jnp.concatenate(weighted, axis=1)
    return lax.dot_general(
        conv_b[skipped:tokens],
        weighted[skipped:tokens],
        (((0,), (0,)), ((), ())),
        preferred_element_type=F32,
    )


B_AT, C_AT = H * P_SIZE // N, H * P_SIZE // N + G


def conv_specs(first, tokens):
    def cols(offset):
        return lambda i: (0, offset + first + i)

    return [
        pl.BlockSpec((tokens, COLS), cols(0)),
        pl.BlockSpec((tokens, N), cols(0)),
        pl.BlockSpec((tokens, N), cols(0)),
        pl.BlockSpec((KERNEL_TAPS, COLS), cols(0)),
        pl.BlockSpec((KERNEL_TAPS, N), cols(B_AT)),
        pl.BlockSpec((KERNEL_TAPS, N), cols(C_AT)),
        pl.BlockSpec((1, tokens, 2 * HEADS), lambda i: (first + i, 0, 0)),
        pl.BlockSpec((2 * HEADS, COLS), lambda i: (0, 0)),
    ]


def rim_specs(first):
    def cols(offset):
        return lambda i: (0, offset + first + i)

    return [
        pl.BlockSpec((RIM, COLS), cols(0)),
        pl.BlockSpec((RIM, N), cols(B_AT)),
        pl.BlockSpec((RIM, N), cols(C_AT)),
    ]


def value_specs(tokens):
    return [pl.BlockSpec((tokens, width), lambda i: (0, i)) for width in (COLS, N, N)]


def value_shapes(count):
    return [jax.ShapeDtypeStruct((SPAN, count * width), BF16) for width in (COLS, N, N)]


def state_outs(first, count):
    rows = count * HALF
    shapes = [(rows, COLS), (rows + log_rows(first), COLS)]
    shapes = [jax.ShapeDtypeStruct(a, BF16) for a in shapes]
    return shapes + [mark()], [whole(a) for a in shapes] + [MARK]


def early_states(first, count, x, b, c, conv_weight, to_end, spread, after):
    def body(*refs):
        outs = refs[8 + len(after) :]
        outs[3][0] = states_body(TILE, refs[:8], outs, outs[-1])
        outs[4][...] = jnp.zeros_like(outs[4])

    return pl.pallas_call(
        body,
        grid=(count,),
        in_specs=conv_specs(first, SPAN) + [corner(a) for a in after],
        out_specs=value_specs(SPAN) + [pl.BlockSpec((1, N, COLS), lambda i: (i, 0, 0)), MARK],
        out_shape=value_shapes(count)
        + [jax.ShapeDtypeStruct((count, N, COLS), F32), mark()],
        scratch_shapes=[pltpu.VMEM((2, PAD + SPAN, 128), F32)],
        compiler_params=params(),
        cost_estimate=cost(1.0),
        name="early_states",
    )(x, b, c, conv_weight, conv_weight, conv_weight, to_end, spread, *after)


def late_states(first, count, early, x, b, c, rim, conv_weight, to_end, spread, flags, last, us):
    values, conv_b, conv_c, partial, token = early

    def body(*refs):
        flag_ref, last_ref, partial_ref = refs[11:14]
        outs = refs[18:]
        state = states_body(0, refs[:11], outs, outs[-1]) + partial_ref[0]
        give_state(state.astype(BF16), pl.program_id(0), flag_ref, last_ref, *outs[3:5])
        outs[5][...] = jnp.zeros_like(outs[5])

    shapes, specs = state_outs(first, count)
    return pl.pallas_call(
        body,
        grid=(count,),
        in_specs=conv_specs(first, TILE)
        + rim_specs(first)
        + [whole(flags), whole(last), pl.BlockSpec((1, N, COLS), lambda i: (i, 0, 0))]
        + [pl.BlockSpec(memory_space=pl.ANY)] * 3
        + [corner(token)],
        out_specs=value_specs(TILE) + specs,
        out_shape=value_shapes(count) + shapes,
        input_output_aliases={14: 0, 15: 1, 16: 2},
        scratch_shapes=[pltpu.VMEM((2, PAD + SPAN, 128), F32)],
        compiler_params=params(),
        cost_estimate=cost(us),
        name="late_states",
    )(
        x, b, c, conv_weight, conv_weight, conv_weight, to_end, spread, rim, rim, rim,
        flags, last, partial, values, conv_b, conv_c, token,
    )


def end_states(first, count, x, b, c, rim, conv_weight, to_end, spread, flags, last, after, us=1.0):
    def body(*refs):
        outs = refs[13 + len(after) :]
        state = states_body(0, refs[:11], outs, outs[-1])
        give_state(state.astype(BF16), pl.program_id(0), *refs[11:13], *outs[3:5])
        outs[5][...] = jnp.zeros_like(outs[5])

    shapes, specs = state_outs(first, count)
    return pl.pallas_call(
        body,
        grid=(count,),
        in_specs=conv_specs(first, SPAN)
        + rim_specs(first)
        + [whole(flags), whole(last)]
        + [corner(a) for a in after],
        out_specs=value_specs(SPAN) + specs,
        out_shape=value_shapes(count) + shapes,
        scratch_shapes=[pltpu.VMEM((2, PAD + SPAN, 128), F32)],
        compiler_params=params(),
        cost_estimate=cost(us),
        name="end_states",
    )(
        x, b, c, conv_weight, conv_weight, conv_weight, to_end, spread, rim, rim, rim,
        flags, last, *after,
    )


def inside_body(values_ref, b_ref, c_ref, cols_ref, rows_ref, skip_ref, part_ref, mark_ref):
    mark_ref[...] = jnp.zeros_like(mark_ref)
    half = SPAN // 2
    scores = lax.dot_general(
        c_ref[...], b_ref[...], (((1,), (1,)), ((), ())), preferred_element_type=F32
    )
    row = lax.broadcasted_iota(jnp.int32, (half, half), 0)
    col = lax.broadcasted_iota(jnp.int32, (half, half), 1)
    causal = row >= col
    lane = lax.broadcasted_iota(jnp.int32, (half, 2 * P_SIZE), 1)
    first_head = lane < P_SIZE
    cols = cols_ref[0]
    rows = rows_ref[...]
    corner, below, later = scores[:half, :half], scores[half:, :half], scores[half:, half:]
    for pair in range(HEADS // 2):
        upper, lower = [], []
        for head in (2 * pair, 2 * pair + 1):
            at_t = cols[:, head : head + 1]
            at_s = rows[head : head + 1, :]
            e = jnp.exp2(at_t[:half] - at_s[:, :half])
            upper.append(jnp.where(causal, corner * e, 0.0).astype(BF16))
            e = jnp.exp2(at_t[half:] - at_s[:, :half])
            left = (below * e).astype(BF16)
            e = jnp.exp2(at_t[half:] - at_s[:, half:])
            right = jnp.where(causal, later * e, 0.0).astype(BF16)
            lower.append(jnp.concatenate([left, right], axis=1))
        sl = slice(pair * 2 * P_SIZE, (pair + 1) * 2 * P_SIZE)
        values = values_ref[:, sl]
        skip = skip_ref[0, :, sl]
        for lo, mix, depth in ((0, upper, half), (half, lower, SPAN)):
            both = jnp.dot(
                jnp.concatenate(mix, axis=0), values[:depth], preferred_element_type=F32
            )
            inside = jnp.where(first_head, both[:half], both[half:])
            part_ref[lo : lo + half, sl] = inside + skip * values[lo : lo + half].astype(F32)


def inside_block(first, count, values, conv_b, conv_c, cols, rows, skip, after, us=1.0):
    def own(i):
        return (0, i)

    return pl.pallas_call(
        lambda *refs: inside_body(*refs[:6], *refs[6 + len(after) :]),
        grid=(count,),
        in_specs=[
            pl.BlockSpec((SPAN, COLS), own),
            pl.BlockSpec((SPAN, N), own),
            pl.BlockSpec((SPAN, N), own),
            pl.BlockSpec((1, SPAN, HEADS), lambda i: (first + i, 0, 0)),
            pl.BlockSpec((HEADS, SPAN), lambda i: (first + i, 0)),
            pl.BlockSpec((1, 1, COLS), lambda i: (first + i, 0, 0)),
        ]
        + [corner(a) for a in after],
        out_specs=[pl.BlockSpec((SPAN, COLS), own), MARK],
        out_shape=[jax.ShapeDtypeStruct((SPAN, count * COLS), F32), mark()],
        compiler_params=params(),
        cost_estimate=cost(us),
        name="inside_block",
    )(values, conv_b, conv_c, cols, rows, skip, *after)


def carried_body(*refs):
    side_ref, c_ref, part_ref, keep_ref, got_ref, from_start_ref, spread_ref = refs[:7]
    out_ref, mark_ref = refs[-2:]
    mark_ref[...] = jnp.zeros_like(mark_ref)
    upper = side_ref[:1] > 0.5
    keep, got = keep_ref[...], got_ref[...]
    carry = jnp.concatenate(
        [jnp.where(upper, got, keep), jnp.where(upper, keep, got)], axis=0
    )
    gain = jnp.dot(from_start_ref[0], spread_ref[...], preferred_element_type=F32)
    carried = jnp.dot(c_ref[...], carry, preferred_element_type=F32)
    out_ref[...] = (part_ref[...] + carried * gain).astype(BF16)


def with_carry(first, count, side, conv_c, part, keep, got, from_start, spread, out, after, us=1.0):
    def own(i):
        return (0, i)

    given = [] if out is None else [out]
    return pl.pallas_call(
        carried_body,
        grid=(count,),
        in_specs=[
            whole(side),
            pl.BlockSpec((SPAN, N), own),
            pl.BlockSpec((SPAN, COLS), own),
            pl.BlockSpec((HALF, COLS), lambda i: (i, 0)),
            pl.BlockSpec((HALF, COLS), lambda i: (i, 0)),
            pl.BlockSpec((1, SPAN, 2 * HEADS), lambda i: (first + i, 0, 0)),
            pl.BlockSpec((2 * HEADS, COLS), lambda i: (0, 0)),
        ]
        + [pl.BlockSpec(memory_space=pl.ANY)] * len(given)
        + [corner(a) for a in after],
        out_specs=[pl.BlockSpec((SPAN, COLS), lambda i: (0, first + i)), MARK],
        out_shape=[jax.ShapeDtypeStruct((SPAN, WIDE), BF16), mark()],
        input_output_aliases={7: 0} if given else {},
        compiler_params=params(),
        cost_estimate=cost(us),
        name="with_carry",
    )(side, conv_c, part, keep, got, from_start, spread, *given, *after)


def swap(value, axis, pairs):
    return lax.ppermute(value, axis, pairs + [(b, a) for a, b in pairs])


def log_rows(first):
    return TILE if first == 0 else 0


def put_log(ref, at, log):
    ref[at:, :] = jnp.zeros((TILE, COLS), BF16)
    parts = []
    for _ in range(3):
        parts.append(log.astype(BF16).astype(F32))
        log = log - parts[-1]
    rest = jnp.zeros((TILE - len(parts), H), F32)
    ref[at:, :H] = jnp.concatenate(parts + [rest], axis=0).astype(BF16)


def take_log(ref, at):
    rows = ref[at:, :H].astype(F32)
    return rows[0:1] + rows[1:2] + rows[2:3]


Y_PAIRS = [(0, 1), (2, 3), (4, 5), (6, 7)]
Z_PAIRS = [(0, 2), (1, 3), (4, 6), (5, 7)]
MID_PAIRS = [(2, 4), (3, 5)]
FAR_PAIRS = [(0, 4), (1, 5), (2, 6), (3, 7)]

ORDER = (
    [("early", 0, 1.0), ("state", 0, 1.0), ("state", 1, 1.0), ("state", 2, 1.0), ("chip", 0, 1.0)]
    + [("state", 3, 1.0), ("chip", 1, 1.0), ("chips", 0, 1.0), ("chip", 2, 1.0)]
    + [("chips", 1, 1.0), ("chip", 3, 1.0), ("link", 0, 1.0), ("chips", 2, 1.0)]
    + [("inside", 0, 1.0), ("inside", 1, 1.0), ("link", 1, 1.0), ("chips", 3, 1.0)]
    + [("inside", 3, 1.0), ("total", 0, 1.0), ("link", 2, 1.0), ("link", 3, 1.0)]
    + [("total", 1, 1.0), ("leave", 0, 1.0), ("inside", 2, 1.0), ("total", 2, 1.0)]
    + [("leave", 1, 1.0), ("out", 0, 1.0), ("total", 3, 1.0), ("leave", 2, 1.0)]
    + [("out", 1, 1.0), ("leave", 3, 1.0), ("out", 2, 1.0), ("out", 3, 1.0)]
)


def places():
    at, core = lax.axis_index("inner"), lax.axis_index("outer")
    z = at >> 1
    row = lax.broadcasted_iota(jnp.int32, (8, COLS), 0)
    flags = jnp.zeros((8, COLS), F32)
    for number, flag in enumerate(((at & 1) == 1, (z & 1) == 1, z >= 2, core == 1)):
        flags = jnp.where((row == number) & flag, 1.0, flags)
    return flags


def merge(body, arrays, weights, lead, flags, spread, after, outs, us):
    count = min(a.shape[0] for a in arrays) // HALF
    rows = count * HALF
    given = [flags, *arrays]
    out = [jax.ShapeDtypeStruct((rows, COLS), BF16)] * outs
    given += weights
    if lead is not None:
        step, known, used, keeps, sends = lead
        asked = [(n, own or at > 0) for own in used for at, n in enumerate(CHUNKS)]
        given += [spread, known]
        if sends:
            out = [jax.ShapeDtypeStruct((rows + TILE, COLS), BF16)]
        out += [jax.ShapeDtypeStruct((8, H), F32)] * keeps
        out += [jax.ShapeDtypeStruct((n, 1, COLS), F32) for n, given_out in asked if given_out]
    out.append(mark())

    def run(*refs):
        ins = refs[1 : 1 + len(arrays)]
        scale_refs = refs[1 + len(arrays) : 1 + len(arrays) + len(weights)]
        rest = refs[1 + len(arrays) + len(weights) : len(given)]
        results = refs[len(given) + len(after) :]
        on = [refs[0][at : at + 1] > 0.5 for at in range(4)]
        results[-1][...] = jnp.zeros((8, 128), F32)
        scales = [[r[at] for r in scale_refs] for at in range(count)]
        if lead is not None:
            logs = [take_log(r, rows) if r.shape[0] > rows else None for r in ins]
            found, kept, onward = step([a[:, :H] for a in on], logs, rest[1][...])
            if keeps:
                empty = jnp.zeros((8 - len(kept), H), F32)
                results[outs][...] = jnp.concatenate(kept + [empty], axis=0)
            if sends:
                put_log(results[0], rows, onward)
            found = [by_column(row, rest[0][...], 2) for row in found]
            scales = [[f[at : at + 1] for f in found] + scales[at] for at in range(count)]
            at = outs + keeps
            first = 0
            for number, (n, given_out) in enumerate(asked):
                value = found[number // len(CHUNKS)]
                first = 0 if number % len(CHUNKS) == 0 else first
                if given_out:
                    for group in range(n):
                        results[at][group] = value[first + group : first + group + 1]
                    at += 1
                first += n
        for at in range(count):
            part = slice(at * HALF, (at + 1) * HALF)
            values = body(on, [r[part, :].astype(F32) for r in ins], scales[at])
            for ref, value in zip(results, values):
                ref[part, :] = value.astype(BF16)

    found = pl.pallas_call(
        run,
        grid=(1,),
        in_specs=[whole(a) for a in given] + [corner(a) for a in after],
        out_specs=[whole(a) for a in out],
        out_shape=out,
        compiler_params=params(),
        cost_estimate=cost(us),
        name=body.__name__,
    )(*given, *after)
    if lead is None:
        return found[:outs], found[-1], None, None
    new = list(found[outs + keeps : -1])
    scales = [new.pop(0) if given_out else None for _, given_out in asked]
    n = len(CHUNKS)
    scales = [scales[n * at : n * (at + 1)] for at in range(len(used))]
    return found[:outs], found[-1], found[outs] if keeps else None, scales


def add_chip(on, arrays, scales):
    upper, _, _, _ = on
    keep, got = arrays
    return (jnp.where(upper, got, keep) * scales[0] + jnp.where(upper, keep, got),)


def chip_logs(on, logs, known):
    upper, _, _, _ = on
    own, got = known[0:1], logs[1]
    low, high = jnp.where(upper, got, own), jnp.where(upper, own, got)
    return [jnp.exp(high), jnp.exp(low)], [low + high], low + high


def add_chips(on, arrays, scales):
    _, odd, _, _ = on
    chip, got = arrays
    return (jnp.where(odd, got, chip) * scales[0] + jnp.where(odd, chip, got),)


def chips_logs(on, logs, known):
    _, odd, _, _ = on
    own, got = known[0:1], logs[1]
    low, high = jnp.where(odd, got, own), jnp.where(odd, own, got)
    return [jnp.exp(high), jnp.exp(own)], [low + high, low], low + high


def go_on(on, arrays, scales):
    _, _, high, _ = on
    chip, two, got = arrays
    own, other, through = scales
    return (jnp.where(high, got * through + chip, two * own + got * other),)


def go_on_logs(on, logs, known):
    _, _, high, _ = on
    own, low, got = known[0:1], known[1:2], logs[2]
    none = jnp.zeros_like(own)
    weights = [jnp.exp(jnp.where(high, none, got)), jnp.exp(jnp.where(high, own, none))]
    return weights, [got, low], got


def add_all(on, arrays, scales):
    _, odd, high, _ = on
    chip, two, got, far = arrays
    own, other, through = scales[:3]
    at_end = jnp.where(high, far * through + chip, far)
    return (jnp.where(odd != high, two * own + got * other, at_end),)


def enter_logs(on, logs, known):
    _, odd, high, core = on
    other, low, further = known[0:1], known[1:2], logs[4]
    none = jnp.zeros_like(other)
    below = jnp.where(odd, low, none)
    reach = jnp.where(high, jnp.where(odd, further, other), none) + below
    return [jnp.where(core, jnp.exp(reach), none)], [], None


def enter(on, arrays, scales):
    upper, odd, high, _ = on
    keep, got_y, got_z, got, far, before = arrays
    reach, below = scales
    low_side = jnp.where(odd, got_z, jnp.zeros_like(got_z))
    entering = jnp.where(high, jnp.where(odd, far, got), low_side) + before * reach
    above = entering * below + jnp.where(upper, got_y, keep)
    return jnp.where(upper, above, entering), jnp.where(upper, entering, above)


def in_order(x, b, c, rim, conv_weight, steps, flags):
    cols, rows, to_end, from_start, last, skip, spread = steps
    starts = [sum(CHUNKS[:k]) for k in range(len(CHUNKS))]
    done, weights = {}, {}
    known = last
    after = []
    out = None

    def merged(body, k, names, scales, logs, wanted, outs=1, sends=True):
        nonlocal known
        lead = None
        if k == 0 and logs is not None:
            used = [name not in ("above", "high", "reach") for name in wanted]
            lead = (logs, known, used, int(sends), sends)
        if lead is None:
            scales = wanted + scales
        found, mark, keeps, new = merge(
            body,
            [done[name, k] for name in names],
            [weights[name][k] for name in scales],
            lead,
            flags,
            spread,
            after,
            outs,
            us,
        )
        if lead is not None:
            known = keeps
            weights.update(zip(wanted, new))
        return found, mark

    for what, k, us in ORDER:
        first, count = starts[k], CHUNKS[k]
        if what == "early":
            early = early_states(first, count, x, b, c, conv_weight, to_end, spread, after)
            done["early", k], mark = early, early[-1]
        elif what == "state":
            given = (x, b, c, rim, conv_weight, to_end, spread, flags, last)
            if ("early", k) in done:
                found = late_states(first, count, done["early", k], *given, us)
            else:
                found = end_states(first, count, *given, after, us)
            done["values", k], done["b", k], done["c", k], keep, send, mark = found
            done["keep", k], done["y", k] = keep, swap(send, "inner", Y_PAIRS)
        elif what == "inside":
            given = [done[name, k] for name in ("values", "b", "c")]
            done["inside", k], mark = inside_block(
                first, count, *given, cols, rows, skip, after, us
            )
        elif what == "chip":
            wanted = ["above", "below"]
            if k > 0:
                wanted = ["above"]
            (found,), mark = merged(add_chip, k, ["keep", "y"], [], chip_logs, wanted)
            done["chip", k], done["z", k] = found, swap(found, "inner", Z_PAIRS)
        elif what == "chips":
            wanted = ["high", "through"]
            if k > 0:
                wanted = ["high"]
            (found,), mark = merged(add_chips, k, ["chip", "z"], [], chips_logs, wanted)
            done["chips", k], done["mid", k] = found, swap(found, "inner", MID_PAIRS)
        elif what == "link":
            names = ["chip", "chips", "mid"]
            (found,), mark = merged(
                go_on, k, names, ["through"], go_on_logs, ["own", "other"]
            )
            done["far", k] = swap(found, "inner", Z_PAIRS)
        elif what == "total":
            names = ["chip", "chips", "mid", "far"]
            (found,), mark = merged(
                add_all, k, names, ["own", "other", "through"], None, []
            )
            done["before", k] = swap(found, "outer", [(0, 1)])
        elif what == "leave":
            names = ["keep", "y", "z", "mid", "far", "before"]
            (stay, leave), mark = merged(
                enter, k, names, ["below"], enter_logs, ["reach"], outs=2, sends=False
            )
            done["stay", k], done["back", k] = stay, swap(leave, "inner", Y_PAIRS)
        else:
            given = [done[name, k] for name in ("c", "inside", "stay", "back")]
            out, mark = with_carry(
                first, count, flags, *given, from_start, spread, out, after, us
            )
        after = [mark]
    return out


def combine(earlier, later):
    return (earlier[0] * later[0], later[0][:, None, :] * earlier[1] + later[1])


def enter_by_all_to_all(last, kept, sent):
    size = lax.axis_size("inner")
    upper = (lax.axis_index("inner") & 1) == 1
    wide = 2 * P_SIZE
    pairs = H // 2
    sent = [a[: b.shape[0]] for a, b in zip(sent, kept)]
    keep, send = [jnp.concatenate(a).reshape(G, HALF, COLS) for a in (kept, sent)]
    halves = [jnp.where(upper, send, keep), jnp.where(upper, keep, send)]
    state = jnp.concatenate(halves, axis=1).reshape(G, N, pairs // G, wide)
    state = jnp.swapaxes(state, 1, 2).reshape(pairs, N, wide)
    decay = jnp.repeat(jnp.exp(last[0]), P_SIZE).reshape(pairs, wide)

    def spread(a):
        return lax.all_to_all(a[None], "inner", split_axis=1, concat_axis=0, tiled=True)

    decays, states = spread(decay), spread(state).astype(F32)
    run = (jnp.ones_like(decays[0]), jnp.zeros_like(states[0]))

    def lap(run, item):
        return combine(run, item), run

    total, before = lax.scan(lap, run, (decays, states))
    first = lax.ppermute(total[1].astype(BF16), "outer", [(0, 1)]).astype(F32)
    entering = before[0][:, :, None, :] * first[None] + before[1]
    carry = lax.all_to_all(
        entering.astype(BF16), "inner", split_axis=0, concat_axis=1, tiled=True
    )[0]
    carry = carry.reshape(G, pairs // G, N, wide)
    carry = jnp.swapaxes(carry, 1, 2).reshape(G, N, COLS)
    top, bottom = carry[:, :HALF], carry[:, HALF:]
    stay, got = jnp.where(upper, bottom, top), jnp.where(upper, top, bottom)
    entered = []
    at = 0
    for count in CHUNKS:
        part = [a[at : at + count].reshape(count * HALF, COLS) for a in (stay, got)]
        entered.append(part)
        at += count
    return entered


def one_by_one(x, b, c, rim, conv_weight, steps, flags):
    cols, rows, to_end, from_start, last, skip, spread = steps
    starts = [sum(CHUNKS[:k]) for k in range(len(CHUNKS))]
    states = [
        end_states(
            first, count, x, b, c, rim, conv_weight, to_end, spread, flags, last, []
        )
        for first, count in zip(starts, CHUNKS)
    ]
    entered = enter_by_all_to_all(last, [a[3] for a in states], [a[4] for a in states])
    out = None
    for first, count, state, (keep, got) in zip(starts, CHUNKS, states, entered):
        values, conv_b, conv_c = state[:3]
        part, _ = inside_block(
            first, count, values, conv_b, conv_c, cols, rows, skip, []
        )
        out, _ = with_carry(
            first, count, flags, conv_c, part, keep, got, from_start, spread, out, []
        )
    return out


def shards(x_stream, b_stream, c_stream, dt_input, decay_log, skip_weight, conv_weight):
    devices = lax.axis_size("outer") * lax.axis_size("inner")
    x_stream, dt_input, flags = lax.optimization_barrier((x_stream, dt_input, places()))
    rim = lax.ppermute(
        rim_rows(x_stream, b_stream, c_stream),
        ("outer", "inner"),
        [(i, i + 1) for i in range(devices - 1)],
    )
    steps = time_steps(dt_input, decay_log, skip_weight)
    by_swaps = lax.axis_size("inner") == 8 and lax.axis_size("outer") == 2
    rest = in_order if by_swaps else one_by_one
    return rest(x_stream, b_stream, c_stream, rim, conv_weight, steps, flags)


def solution(mesh):
    return jax.shard_map(
        shards,
        mesh=mesh,
        in_specs=(
            P(("slab", "outer", "inner"), None),
            P(("slab", "outer", "inner"), None),
            P(("slab", "outer", "inner"), None),
            P(("slab", "outer", "inner"), None),
            P("slab"),
            P(),
            P(),
        ),
        out_specs=P(("slab", "outer", "inner"), None),
        check_vma=False,
    )
```

```python
import jax
import jax.numpy as jnp
from jax import lax
from jax.experimental import pallas as pl
from jax.experimental.pallas import tpu as pltpu
from jax.sharding import PartitionSpec as P

H = 128
P_SIZE = 64
N = 128
G = 8
KERNEL_TAPS = 4
SPAN = 256

HEADS = H // G
COLS = HEADS * P_SIZE
HALF = N // 2
RIM = KERNEL_TAPS - 1
PAD = 8
LOG2E = 1.4426950408889634
VMEM = 16 * 1024 * 1024
TILE = 16
WIDE = H * P_SIZE
F32 = jnp.float32
BF16 = jnp.bfloat16
CHUNKS = (2, 2, 2, 2)


def params():
    return pltpu.CompilerParams(vmem_limit_bytes=VMEM)


def cost(us, moved=0):
    return pl.CostEstimate(flops=int(us * 6e8), bytes_accessed=moved, transcendentals=0)


def mark():
    return jax.ShapeDtypeStruct((8, 128), F32)


MARK = pl.BlockSpec((8, 128), lambda i: (0, 0))


def corner(a):
    tile = tuple(min(n, m) for n, m in zip(a.shape[-2:], (TILE, 128)))
    block = (1,) * (a.ndim - 2) + tile
    return pl.BlockSpec(block, lambda i: (0,) * a.ndim)


def rim_body(x_ref, b_ref, c_ref, rim_ref):
    rim_ref[:, :WIDE] = x_ref[TILE - RIM :, :]
    rim_ref[:, WIDE : WIDE + G * N] = b_ref[TILE - RIM :, :]
    rim_ref[:, WIDE + G * N :] = c_ref[TILE - RIM :, :]


def rim_rows(x, b, c):
    at = x.shape[0] // TILE - 1
    width = x.shape[1] + b.shape[1] + c.shape[1]
    return pl.pallas_call(
        rim_body,
        grid=(1,),
        in_specs=[pl.BlockSpec((TILE, a.shape[1]), lambda i: (at, 0)) for a in (x, b, c)],
        out_specs=pl.BlockSpec((RIM, width), lambda i: (0, 0)),
        out_shape=jax.ShapeDtypeStruct((RIM, width), BF16),
        compiler_params=params(),
        cost_estimate=cost(1.0),
        name="rim_rows",
    )(*[pltpu.with_memory_space_constraint(a, pltpu.HBM) for a in (x, b, c)])


def whole(a):
    return pl.BlockSpec(a.shape, lambda i: (0,) * len(a.shape))


def split(value, parts):
    found = []
    for _ in range(parts):
        found.append(value.astype(BF16))
        value = value - found[-1].astype(F32)
    groups = []
    for group in range(G):
        lo = group * HEADS
        groups.append(jnp.concatenate([a[:, lo : lo + HEADS] for a in found], axis=1))
    return groups


def spreader(parts):
    head = lax.broadcasted_iota(jnp.int32, (parts * HEADS, COLS), 0) % HEADS
    col = lax.broadcasted_iota(jnp.int32, (parts * HEADS, COLS), 1) // P_SIZE
    return jnp.where(head == col, 1.0, 0.0).astype(BF16)


def by_column(value, matrix, parts):
    rows = jnp.concatenate(split(value, parts), axis=0)
    return jnp.dot(rows, matrix, preferred_element_type=F32)


def steps_body(
    dt_ref,
    decay_ref,
    skip_ref,
    cols_ref,
    rows_ref,
    to_end_ref,
    from_start_ref,
    last_ref,
    skip_cols_ref,
    spread_ref,
):
    raw = dt_ref[...].astype(F32)
    dt = jnp.maximum(raw, 0.0) + jnp.log1p(jnp.exp(-jnp.abs(raw)))
    step = dt * (-jnp.exp(decay_ref[...]))
    row = lax.broadcasted_iota(jnp.int32, (SPAN, SPAN), 0)
    col = lax.broadcasted_iota(jnp.int32, (SPAN, SPAN), 1)
    tri = jnp.where(row >= col, 1.0, 0.0).astype(F32)
    cum = jnp.dot(tri, step, precision=lax.Precision.HIGHEST, preferred_element_type=F32)
    last = cum[SPAN - 1 :, :]
    last_ref[...] = last
    rows_ref[...] = jnp.transpose((cum - jnp.log(dt)) * LOG2E)
    to_end = split(jnp.exp(last - cum) * dt, 2)
    from_start = split(jnp.exp(cum), 2)
    scaled = cum * LOG2E
    for group in range(G):
        lo = group * HEADS
        cols_ref[group] = scaled[:, lo : lo + HEADS]
        to_end_ref[group] = to_end[group]
        from_start_ref[group] = from_start[group]
    skip_cols = by_column(skip_ref[...], spreader(3), 3)
    for group in range(G):
        skip_cols_ref[group] = skip_cols[group : group + 1]
    spread_ref[...] = spreader(2)


def time_steps(dt_input, decay_log, skip_weight):
    given = (dt_input, decay_log.reshape(1, H), skip_weight.reshape(1, H))
    out = [
        jax.ShapeDtypeStruct((G, SPAN, HEADS), F32),
        jax.ShapeDtypeStruct((H, SPAN), F32),
        jax.ShapeDtypeStruct((G, SPAN, 2 * HEADS), BF16),
        jax.ShapeDtypeStruct((G, SPAN, 2 * HEADS), BF16),
        jax.ShapeDtypeStruct((1, H), F32),
        jax.ShapeDtypeStruct((G, 1, COLS), F32),
        jax.ShapeDtypeStruct((2 * HEADS, COLS), BF16),
    ]
    return pl.pallas_call(
        steps_body,
        grid=(1,),
        in_specs=[whole(a) for a in given],
        out_specs=[whole(a) for a in out],
        out_shape=out,
        compiler_params=params(),
        cost_estimate=cost(2.0),
        name="time_steps",
    )(*given)


def convolved(now, rim, kernel, scratch):
    kernel = kernel.astype(F32) * 0.5
    tokens = now.shape[0]
    now = now.astype(F32)
    scratch[PAD - RIM : PAD, :] = rim.astype(F32)
    scratch[PAD : PAD + tokens, :] = now
    half = kernel[RIM : RIM + 1] * now
    for tap in range(RIM):
        first = PAD - RIM + tap
        half = half + kernel[tap : tap + 1] * scratch[first : first + tokens, :]
    return (half + half * jnp.tanh(half)).astype(BF16)


def give_state(state, at, flag_ref, last_ref, keep_ref, send_ref):
    upper = flag_ref[:1] > 0.5
    rows = pl.ds(pl.multiple_of(at * HALF, HALF), HALF)
    keep_ref[rows, :] = jnp.where(upper, state[HALF:], state[:HALF])
    send_ref[rows, :] = jnp.where(upper, state[:HALF], state[HALF:])
    if send_ref.shape[0] > keep_ref.shape[0]:
        put_log(send_ref, keep_ref.shape[0], last_ref[...])


def states_body(skipped, given, outs, scratch):
    x_ref, b_ref, c_ref, kernel_x_ref, kernel_b_ref, kernel_c_ref, to_end_ref, spread_ref = given[:8]
    values_ref, conv_b_ref, conv_c_ref = outs[:3]
    rims = given[8:11] if not skipped else [None] * 3
    tokens = x_ref.shape[0]

    def conv(ref, rim_ref, kernel_ref, lo, turn):
        sl = slice(lo, lo + 128)
        rim = jnp.zeros((RIM, 128), F32) if rim_ref is None else rim_ref[:, sl]
        return convolved(ref[:, sl], rim, kernel_ref[:, sl], scratch.at[turn])

    conv_b = conv(b_ref, rims[1], kernel_b_ref, 0, 0)
    conv_b_ref[...] = conv_b
    conv_c_ref[...] = conv(c_ref, rims[2], kernel_c_ref, 0, 1)
    gain = jnp.dot(to_end_ref[0], spread_ref[...], preferred_element_type=F32)
    weighted = []
    for at in range(x_ref.shape[1] // 128):
        sl = slice(at * 128, (at + 1) * 128)
        part = conv(x_ref, rims[0], kernel_x_ref, at * 128, at % 2)
        values_ref[:, sl] = part
        weighted.append((part.astype(F32) * gain[:, sl]).astype(BF16))
    weighted = jnp.concatenate(weighted, axis=1)
    return lax.dot_general(
        conv_b[skipped:tokens],
        weighted[skipped:tokens],
        (((0,), (0,)), ((), ())),
        preferred_element_type=F32,
    )


B_AT, C_AT = H * P_SIZE // N, H * P_SIZE // N + G


def conv_specs(first, tokens):
    def cols(offset):
        return lambda i: (0, offset + first + i)

    return [
        pl.BlockSpec((tokens, COLS), cols(0)),
        pl.BlockSpec((tokens, N), cols(0)),
        pl.BlockSpec((tokens, N), cols(0)),
        pl.BlockSpec((KERNEL_TAPS, COLS), cols(0)),
        pl.BlockSpec((KERNEL_TAPS, N), cols(B_AT)),
        pl.BlockSpec((KERNEL_TAPS, N), cols(C_AT)),
        pl.BlockSpec((1, tokens, 2 * HEADS), lambda i: (first + i, 0, 0)),
        pl.BlockSpec((2 * HEADS, COLS), lambda i: (0, 0)),
    ]


def rim_specs(first):
    def cols(offset):
        return lambda i: (0, offset + first + i)

    return [
        pl.BlockSpec((RIM, COLS), cols(0)),
        pl.BlockSpec((RIM, N), cols(B_AT)),
        pl.BlockSpec((RIM, N), cols(C_AT)),
    ]


def value_specs(tokens):
    return [pl.BlockSpec((tokens, width), lambda i: (0, i)) for width in (COLS, N, N)]


def value_shapes(count):
    return [jax.ShapeDtypeStruct((SPAN, count * width), BF16) for width in (COLS, N, N)]


def state_outs(first, count):
    rows = count * HALF
    shapes = [(rows, COLS), (rows + log_rows(first), COLS)]
    shapes = [jax.ShapeDtypeStruct(a, BF16) for a in shapes]
    return shapes + [mark()], [whole(a) for a in shapes] + [MARK]


def early_states(first, count, x, b, c, conv_weight, to_end, spread, after):
    def body(*refs):
        outs = refs[8 + len(after) :]
        outs[3][0] = states_body(TILE, refs[:8], outs, outs[-1])
        outs[4][...] = jnp.zeros_like(outs[4])

    return pl.pallas_call(
        body,
        grid=(count,),
        in_specs=conv_specs(first, SPAN) + [corner(a) for a in after],
        out_specs=value_specs(SPAN) + [pl.BlockSpec((1, N, COLS), lambda i: (i, 0, 0)), MARK],
        out_shape=value_shapes(count)
        + [jax.ShapeDtypeStruct((count, N, COLS), F32), mark()],
        scratch_shapes=[pltpu.VMEM((2, PAD + SPAN, 128), F32)],
        compiler_params=params(),
        cost_estimate=cost(1.0),
        name="early_states",
    )(x, b, c, conv_weight, conv_weight, conv_weight, to_end, spread, *after)


def late_states(first, count, early, x, b, c, rim, conv_weight, to_end, spread, flags, last, us):
    values, conv_b, conv_c, partial, token = early

    def body(*refs):
        flag_ref, last_ref, partial_ref = refs[11:14]
        outs = refs[18:]
        state = states_body(0, refs[:11], outs, outs[-1]) + partial_ref[0]
        give_state(state.astype(BF16), pl.program_id(0), flag_ref, last_ref, *outs[3:5])
        outs[5][...] = jnp.zeros_like(outs[5])

    shapes, specs = state_outs(first, count)
    return pl.pallas_call(
        body,
        grid=(count,),
        in_specs=conv_specs(first, TILE)
        + rim_specs(first)
        + [whole(flags), whole(last), pl.BlockSpec((1, N, COLS), lambda i: (i, 0, 0))]
        + [pl.BlockSpec(memory_space=pl.ANY)] * 3
        + [corner(token)],
        out_specs=value_specs(TILE) + specs,
        out_shape=value_shapes(count) + shapes,
        input_output_aliases={14: 0, 15: 1, 16: 2},
        scratch_shapes=[pltpu.VMEM((2, PAD + SPAN, 128), F32)],
        compiler_params=params(),
        cost_estimate=cost(us),
        name="late_states",
    )(
        x, b, c, conv_weight, conv_weight, conv_weight, to_end, spread, rim, rim, rim,
        flags, last, partial, values, conv_b, conv_c, token,
    )


def end_states(first, count, x, b, c, rim, conv_weight, to_end, spread, flags, last, after, us=1.0):
    def body(*refs):
        outs = refs[13 + len(after) :]
        state = states_body(0, refs[:11], outs, outs[-1])
        give_state(state.astype(BF16), pl.program_id(0), *refs[11:13], *outs[3:5])
        outs[5][...] = jnp.zeros_like(outs[5])

    shapes, specs = state_outs(first, count)
    return pl.pallas_call(
        body,
        grid=(count,),
        in_specs=conv_specs(first, SPAN)
        + rim_specs(first)
        + [whole(flags), whole(last)]
        + [corner(a) for a in after],
        out_specs=value_specs(SPAN) + specs,
        out_shape=value_shapes(count) + shapes,
        scratch_shapes=[pltpu.VMEM((2, PAD + SPAN, 128), F32)],
        compiler_params=params(),
        cost_estimate=cost(us),
        name="end_states",
    )(
        x, b, c, conv_weight, conv_weight, conv_weight, to_end, spread, rim, rim, rim,
        flags, last, *after,
    )


def inside_body(values_ref, b_ref, c_ref, cols_ref, rows_ref, skip_ref, part_ref, mark_ref):
    mark_ref[...] = jnp.zeros_like(mark_ref)
    half = SPAN // 2
    scores = lax.dot_general(
        c_ref[...], b_ref[...], (((1,), (1,)), ((), ())), preferred_element_type=F32
    )
    row = lax.broadcasted_iota(jnp.int32, (half, half), 0)
    col = lax.broadcasted_iota(jnp.int32, (half, half), 1)
    causal = row >= col
    lane = lax.broadcasted_iota(jnp.int32, (half, 2 * P_SIZE), 1)
    first_head = lane < P_SIZE
    cols = cols_ref[0]
    rows = rows_ref[...]
    corner, below, later = scores[:half, :half], scores[half:, :half], scores[half:, half:]
    for pair in range(HEADS // 2):
        upper, lower = [], []
        for head in (2 * pair, 2 * pair + 1):
            at_t = cols[:, head : head + 1]
            at_s = rows[head : head + 1, :]
            e = jnp.exp2(at_t[:half] - at_s[:, :half])
            upper.append(jnp.where(causal, corner * e, 0.0).astype(BF16))
            e = jnp.exp2(at_t[half:] - at_s[:, :half])
            left = (below * e).astype(BF16)
            e = jnp.exp2(at_t[half:] - at_s[:, half:])
            right = jnp.where(causal, later * e, 0.0).astype(BF16)
            lower.append(jnp.concatenate([left, right], axis=1))
        sl = slice(pair * 2 * P_SIZE, (pair + 1) * 2 * P_SIZE)
        values = values_ref[:, sl]
        skip = skip_ref[0, :, sl]
        for lo, mix, depth in ((0, upper, half), (half, lower, SPAN)):
            both = jnp.dot(
                jnp.concatenate(mix, axis=0), values[:depth], preferred_element_type=F32
            )
            inside = jnp.where(first_head, both[:half], both[half:])
            part_ref[lo : lo + half, sl] = inside + skip * values[lo : lo + half].astype(F32)


def inside_block(first, count, values, conv_b, conv_c, cols, rows, skip, after, us=1.0):
    def own(i):
        return (0, i)

    return pl.pallas_call(
        lambda *refs: inside_body(*refs[:6], *refs[6 + len(after) :]),
        grid=(count,),
        in_specs=[
            pl.BlockSpec((SPAN, COLS), own),
            pl.BlockSpec((SPAN, N), own),
            pl.BlockSpec((SPAN, N), own),
            pl.BlockSpec((1, SPAN, HEADS), lambda i: (first + i, 0, 0)),
            pl.BlockSpec((HEADS, SPAN), lambda i: (first + i, 0)),
            pl.BlockSpec((1, 1, COLS), lambda i: (first + i, 0, 0)),
        ]
        + [corner(a) for a in after],
        out_specs=[pl.BlockSpec((SPAN, COLS), own), MARK],
        out_shape=[jax.ShapeDtypeStruct((SPAN, count * COLS), F32), mark()],
        compiler_params=params(),
        cost_estimate=cost(us),
        name="inside_block",
    )(values, conv_b, conv_c, cols, rows, skip, *after)


def carried_body(*refs):
    side_ref, c_ref, part_ref, keep_ref, got_ref, from_start_ref, spread_ref = refs[:7]
    out_ref, mark_ref = refs[-2:]
    mark_ref[...] = jnp.zeros_like(mark_ref)
    upper = side_ref[:1] > 0.5
    keep, got = keep_ref[...], got_ref[...]
    carry = jnp.concatenate(
        [jnp.where(upper, got, keep), jnp.where(upper, keep, got)], axis=0
    )
    gain = jnp.dot(from_start_ref[0], spread_ref[...], preferred_element_type=F32)
    carried = jnp.dot(c_ref[...], carry, preferred_element_type=F32)
    out_ref[...] = (part_ref[...] + carried * gain).astype(BF16)


def with_carry(first, count, side, conv_c, part, keep, got, from_start, spread, out, after, us=1.0):
    def own(i):
        return (0, i)

    given = [] if out is None else [out]
    return pl.pallas_call(
        carried_body,
        grid=(count,),
        in_specs=[
            whole(side),
            pl.BlockSpec((SPAN, N), own),
            pl.BlockSpec((SPAN, COLS), own),
            pl.BlockSpec((HALF, COLS), lambda i: (i, 0)),
            pl.BlockSpec((HALF, COLS), lambda i: (i, 0)),
            pl.BlockSpec((1, SPAN, 2 * HEADS), lambda i: (first + i, 0, 0)),
            pl.BlockSpec((2 * HEADS, COLS), lambda i: (0, 0)),
        ]
        + [pl.BlockSpec(memory_space=pl.ANY)] * len(given)
        + [corner(a) for a in after],
        out_specs=[pl.BlockSpec((SPAN, COLS), lambda i: (0, first + i)), MARK],
        out_shape=[jax.ShapeDtypeStruct((SPAN, WIDE), BF16), mark()],
        input_output_aliases={7: 0} if given else {},
        compiler_params=params(),
        cost_estimate=cost(us),
        name="with_carry",
    )(side, conv_c, part, keep, got, from_start, spread, *given, *after)


def swap(value, axis, pairs):
    return lax.ppermute(value, axis, pairs + [(b, a) for a, b in pairs])


def log_rows(first):
    return TILE if first == 0 else 0


def put_log(ref, at, log):
    ref[at:, :] = jnp.zeros((TILE, COLS), BF16)
    parts = []
    for _ in range(3):
        parts.append(log.astype(BF16).astype(F32))
        log = log - parts[-1]
    rest = jnp.zeros((TILE - len(parts), H), F32)
    ref[at:, :H] = jnp.concatenate(parts + [rest], axis=0).astype(BF16)


def take_log(ref, at):
    rows = ref[at:, :H].astype(F32)
    return rows[0:1] + rows[1:2] + rows[2:3]


Y_PAIRS = [(0, 1), (2, 3), (4, 5), (6, 7)]
Z_PAIRS = [(0, 2), (1, 3), (4, 6), (5, 7)]
MID_PAIRS = [(2, 4), (3, 5)]
FAR_PAIRS = [(0, 4), (1, 5), (2, 6), (3, 7)]

ORDER = (
    [("early", 0, 1.0), ("state", 0, 1.0), ("state", 1, 1.0), ("state", 2, 1.0), ("chip", 0, 1.0)]
    + [("state", 3, 1.0), ("chip", 1, 1.0), ("chips", 0, 1.0), ("chip", 2, 1.0)]
    + [("chips", 1, 1.0), ("chip", 3, 1.0), ("inside", 0, 1.0), ("link", 0, 1.0)]
    + [("chips", 2, 1.0), ("link", 1, 1.0), ("chips", 3, 1.0), ("inside", 1, 1.0)]
    + [("total", 0, 1.0), ("link", 2, 1.0), ("link", 3, 1.0), ("total", 1, 1.0)]
    + [("leave", 0, 1.0), ("total", 2, 1.0), ("leave", 1, 1.0), ("out", 0, 1.0)]
    + [("total", 3, 1.0), ("leave", 2, 1.0), ("out", 1, 1.0), ("leave", 3, 1.0)]
    + [("inside", 2, 1.0), ("inside", 3, 1.0), ("out", 2, 1.0), ("out", 3, 1.0)]
)


def places():
    at, core = lax.axis_index("inner"), lax.axis_index("outer")
    z = at >> 1
    row = lax.broadcasted_iota(jnp.int32, (8, COLS), 0)
    flags = jnp.zeros((8, COLS), F32)
    for number, flag in enumerate(((at & 1) == 1, (z & 1) == 1, z >= 2, core == 1)):
        flags = jnp.where((row == number) & flag, 1.0, flags)
    return flags


def merge(body, arrays, weights, lead, flags, spread, after, outs, us):
    count = min(a.shape[0] for a in arrays) // HALF
    rows = count * HALF
    given = [flags, *arrays]
    out = [jax.ShapeDtypeStruct((rows, COLS), BF16)] * outs
    given += weights
    if lead is not None:
        step, known, used, keeps, sends = lead
        asked = [(n, own or at > 0) for own in used for at, n in enumerate(CHUNKS)]
        given += [spread, known]
        if sends:
            out = [jax.ShapeDtypeStruct((rows + TILE, COLS), BF16)]
        out += [jax.ShapeDtypeStruct((8, H), F32)] * keeps
        out += [jax.ShapeDtypeStruct((n, 1, COLS), F32) for n, given_out in asked if given_out]
    out.append(mark())

    def run(*refs):
        ins = refs[1 : 1 + len(arrays)]
        scale_refs = refs[1 + len(arrays) : 1 + len(arrays) + len(weights)]
        rest = refs[1 + len(arrays) + len(weights) : len(given)]
        results = refs[len(given) + len(after) :]
        on = [refs[0][at : at + 1] > 0.5 for at in range(4)]
        results[-1][...] = jnp.zeros((8, 128), F32)
        scales = [[r[at] for r in scale_refs] for at in range(count)]
        if lead is not None:
            logs = [take_log(r, rows) if r.shape[0] > rows else None for r in ins]
            found, kept, onward = step([a[:, :H] for a in on], logs, rest[1][...])
            if keeps:
                empty = jnp.zeros((8 - len(kept), H), F32)
                results[outs][...] = jnp.concatenate(kept + [empty], axis=0)
            if sends:
                put_log(results[0], rows, onward)
            found = [by_column(row, rest[0][...], 2) for row in found]
            scales = [[f[at : at + 1] for f in found] + scales[at] for at in range(count)]
            at = outs + keeps
            first = 0
            for number, (n, given_out) in enumerate(asked):
                value = found[number // len(CHUNKS)]
                first = 0 if number % len(CHUNKS) == 0 else first
                if given_out:
                    for group in range(n):
                        results[at][group] = value[first + group : first + group + 1]
                    at += 1
                first += n
        for at in range(count):
            part = slice(at * HALF, (at + 1) * HALF)
            values = body(on, [r[part, :].astype(F32) for r in ins], scales[at])
            for ref, value in zip(results, values):
                ref[part, :] = value.astype(BF16)

    found = pl.pallas_call(
        run,
        grid=(1,),
        in_specs=[whole(a) for a in given] + [corner(a) for a in after],
        out_specs=[whole(a) for a in out],
        out_shape=out,
        compiler_params=params(),
        cost_estimate=cost(us),
        name=body.__name__,
    )(*given, *after)
    if lead is None:
        return found[:outs], found[-1], None, None
    new = list(found[outs + keeps : -1])
    scales = [new.pop(0) if given_out else None for _, given_out in asked]
    n = len(CHUNKS)
    scales = [scales[n * at : n * (at + 1)] for at in range(len(used))]
    return found[:outs], found[-1], found[outs] if keeps else None, scales


def add_chip(on, arrays, scales):
    upper, _, _, _ = on
    keep, got = arrays
    return (jnp.where(upper, got, keep) * scales[0] + jnp.where(upper, keep, got),)


def chip_logs(on, logs, known):
    upper, _, _, _ = on
    own, got = known[0:1], logs[1]
    low, high = jnp.where(upper, got, own), jnp.where(upper, own, got)
    return [jnp.exp(high), jnp.exp(low)], [low + high], low + high


def add_chips(on, arrays, scales):
    _, odd, _, _ = on
    chip, got = arrays
    return (jnp.where(odd, got, chip) * scales[0] + jnp.where(odd, chip, got),)


def chips_logs(on, logs, known):
    _, odd, _, _ = on
    own, got = known[0:1], logs[1]
    low, high = jnp.where(odd, got, own), jnp.where(odd, own, got)
    return [jnp.exp(high), jnp.exp(own)], [low + high, low], low + high


def go_on(on, arrays, scales):
    _, _, high, _ = on
    chip, two, got = arrays
    own, other, through = scales
    return (jnp.where(high, got * through + chip, two * own + got * other),)


def go_on_logs(on, logs, known):
    _, _, high, _ = on
    own, low, got = known[0:1], known[1:2], logs[2]
    none = jnp.zeros_like(own)
    weights = [jnp.exp(jnp.where(high, none, got)), jnp.exp(jnp.where(high, own, none))]
    return weights, [got, low], got


def add_all(on, arrays, scales):
    _, odd, high, _ = on
    chip, two, got, far = arrays
    own, other, through = scales[:3]
    at_end = jnp.where(high, far * through + chip, far)
    return (jnp.where(odd != high, two * own + got * other, at_end),)


def enter_logs(on, logs, known):
    _, odd, high, core = on
    other, low, further = known[0:1], known[1:2], logs[4]
    none = jnp.zeros_like(other)
    below = jnp.where(odd, low, none)
    reach = jnp.where(high, jnp.where(odd, further, other), none) + below
    return [jnp.where(core, jnp.exp(reach), none)], [], None


def enter(on, arrays, scales):
    upper, odd, high, _ = on
    keep, got_y, got_z, got, far, before = arrays
    reach, below = scales
    low_side = jnp.where(odd, got_z, jnp.zeros_like(got_z))
    entering = jnp.where(high, jnp.where(odd, far, got), low_side) + before * reach
    above = entering * below + jnp.where(upper, got_y, keep)
    return jnp.where(upper, above, entering), jnp.where(upper, entering, above)


def in_order(x, b, c, rim, conv_weight, steps, flags):
    cols, rows, to_end, from_start, last, skip, spread = steps
    starts = [sum(CHUNKS[:k]) for k in range(len(CHUNKS))]
    done, weights = {}, {}
    known = last
    after = []
    out = None

    def merged(body, k, names, scales, logs, wanted, outs=1, sends=True):
        nonlocal known
        lead = None
        if k == 0 and logs is not None:
            used = [name not in ("above", "high", "reach") for name in wanted]
            lead = (logs, known, used, int(sends), sends)
        if lead is None:
            scales = wanted + scales
        found, mark, keeps, new = merge(
            body,
            [done[name, k] for name in names],
            [weights[name][k] for name in scales],
            lead,
            flags,
            spread,
            after,
            outs,
            us,
        )
        if lead is not None:
            known = keeps
            weights.update(zip(wanted, new))
        return found, mark

    for what, k, us in ORDER:
        first, count = starts[k], CHUNKS[k]
        if what == "early":
            early = early_states(first, count, x, b, c, conv_weight, to_end, spread, after)
            done["early", k], mark = early, early[-1]
        elif what == "state":
            given = (x, b, c, rim, conv_weight, to_end, spread, flags, last)
            if ("early", k) in done:
                found = late_states(first, count, done["early", k], *given, us)
            else:
                found = end_states(first, count, *given, after, us)
            done["values", k], done["b", k], done["c", k], keep, send, mark = found
            done["keep", k], done["y", k] = keep, swap(send, "inner", Y_PAIRS)
        elif what == "inside":
            given = [done[name, k] for name in ("values", "b", "c")]
            done["inside", k], mark = inside_block(
                first, count, *given, cols, rows, skip, after, us
            )
        elif what == "chip":
            wanted = ["above", "below"]
            if k > 0:
                wanted = ["above"]
            (found,), mark = merged(add_chip, k, ["keep", "y"], [], chip_logs, wanted)
            done["chip", k], done["z", k] = found, swap(found, "inner", Z_PAIRS)
        elif what == "chips":
            wanted = ["high", "through"]
            if k > 0:
                wanted = ["high"]
            (found,), mark = merged(add_chips, k, ["chip", "z"], [], chips_logs, wanted)
            done["chips", k], done["mid", k] = found, swap(found, "inner", MID_PAIRS)
        elif what == "link":
            names = ["chip", "chips", "mid"]
            (found,), mark = merged(
                go_on, k, names, ["through"], go_on_logs, ["own", "other"]
            )
            done["far", k] = swap(found, "inner", Z_PAIRS)
        elif what == "total":
            names = ["chip", "chips", "mid", "far"]
            (found,), mark = merged(
                add_all, k, names, ["own", "other", "through"], None, []
            )
            done["before", k] = swap(found, "outer", [(0, 1)])
        elif what == "leave":
            names = ["keep", "y", "z", "mid", "far", "before"]
            (stay, leave), mark = merged(
                enter, k, names, ["below"], enter_logs, ["reach"], outs=2, sends=False
            )
            done["stay", k], done["back", k] = stay, swap(leave, "inner", Y_PAIRS)
        else:
            given = [done[name, k] for name in ("c", "inside", "stay", "back")]
            out, mark = with_carry(
                first, count, flags, *given, from_start, spread, out, after, us
            )
        after = [mark]
    return out


def combine(earlier, later):
    return (earlier[0] * later[0], later[0][:, None, :] * earlier[1] + later[1])


def enter_by_all_to_all(last, kept, sent):
    size = lax.axis_size("inner")
    upper = (lax.axis_index("inner") & 1) == 1
    wide = 2 * P_SIZE
    pairs = H // 2
    sent = [a[: b.shape[0]] for a, b in zip(sent, kept)]
    keep, send = [jnp.concatenate(a).reshape(G, HALF, COLS) for a in (kept, sent)]
    halves = [jnp.where(upper, send, keep), jnp.where(upper, keep, send)]
    state = jnp.concatenate(halves, axis=1).reshape(G, N, pairs // G, wide)
    state = jnp.swapaxes(state, 1, 2).reshape(pairs, N, wide)
    decay = jnp.repeat(jnp.exp(last[0]), P_SIZE).reshape(pairs, wide)

    def spread(a):
        return lax.all_to_all(a[None], "inner", split_axis=1, concat_axis=0, tiled=True)

    decays, states = spread(decay), spread(state).astype(F32)
    run = (jnp.ones_like(decays[0]), jnp.zeros_like(states[0]))

    def lap(run, item):
        return combine(run, item), run

    total, before = lax.scan(lap, run, (decays, states))
    first = lax.ppermute(total[1].astype(BF16), "outer", [(0, 1)]).astype(F32)
    entering = before[0][:, :, None, :] * first[None] + before[1]
    carry = lax.all_to_all(
        entering.astype(BF16), "inner", split_axis=0, concat_axis=1, tiled=True
    )[0]
    carry = carry.reshape(G, pairs // G, N, wide)
    carry = jnp.swapaxes(carry, 1, 2).reshape(G, N, COLS)
    top, bottom = carry[:, :HALF], carry[:, HALF:]
    stay, got = jnp.where(upper, bottom, top), jnp.where(upper, top, bottom)
    entered = []
    at = 0
    for count in CHUNKS:
        part = [a[at : at + count].reshape(count * HALF, COLS) for a in (stay, got)]
        entered.append(part)
        at += count
    return entered


def one_by_one(x, b, c, rim, conv_weight, steps, flags):
    cols, rows, to_end, from_start, last, skip, spread = steps
    starts = [sum(CHUNKS[:k]) for k in range(len(CHUNKS))]
    states = [
        end_states(
            first, count, x, b, c, rim, conv_weight, to_end, spread, flags, last, []
        )
        for first, count in zip(starts, CHUNKS)
    ]
    entered = enter_by_all_to_all(last, [a[3] for a in states], [a[4] for a in states])
    out = None
    for first, count, state, (keep, got) in zip(starts, CHUNKS, states, entered):
        values, conv_b, conv_c = state[:3]
        part, _ = inside_block(
            first, count, values, conv_b, conv_c, cols, rows, skip, []
        )
        out, _ = with_carry(
            first, count, flags, conv_c, part, keep, got, from_start, spread, out, []
        )
    return out


def shards(x_stream, b_stream, c_stream, dt_input, decay_log, skip_weight, conv_weight):
    devices = lax.axis_size("outer") * lax.axis_size("inner")
    x_stream, dt_input, flags = lax.optimization_barrier((x_stream, dt_input, places()))
    rim = lax.ppermute(
        rim_rows(x_stream, b_stream, c_stream),
        ("outer", "inner"),
        [(i, i + 1) for i in range(devices - 1)],
    )
    steps = time_steps(dt_input, decay_log, skip_weight)
    by_swaps = lax.axis_size("inner") == 8 and lax.axis_size("outer") == 2
    rest = in_order if by_swaps else one_by_one
    return rest(x_stream, b_stream, c_stream, rim, conv_weight, steps, flags)


def solution(mesh):
    return jax.shard_map(
        shards,
        mesh=mesh,
        in_specs=(
            P(("slab", "outer", "inner"), None),
            P(("slab", "outer", "inner"), None),
            P(("slab", "outer", "inner"), None),
            P(("slab", "outer", "inner"), None),
            P("slab"),
            P(),
            P(),
        ),
        out_specs=P(("slab", "outer", "inner"), None),
        check_vma=False,
    )
```

```python
import jax
import jax.numpy as jnp
from jax import lax
from jax.experimental import pallas as pl
from jax.experimental.pallas import tpu as pltpu
from jax.sharding import PartitionSpec as P

H = 128
P_SIZE = 64
N = 128
G = 8
KERNEL_TAPS = 4
SPAN = 256

HEADS = H // G
COLS = HEADS * P_SIZE
HALF = N // 2
RIM = KERNEL_TAPS - 1
PAD = 8
LOG2E = 1.4426950408889634
VMEM = 16 * 1024 * 1024
TILE = 16
WIDE = H * P_SIZE
F32 = jnp.float32
BF16 = jnp.bfloat16
CHUNKS = (2, 2, 2, 2)


def params():
    return pltpu.CompilerParams(vmem_limit_bytes=VMEM)


def cost(us, moved=0):
    return pl.CostEstimate(flops=int(us * 6e8), bytes_accessed=moved, transcendentals=0)


def mark():
    return jax.ShapeDtypeStruct((8, 128), F32)


MARK = pl.BlockSpec((8, 128), lambda i: (0, 0))


def corner(a):
    tile = tuple(min(n, m) for n, m in zip(a.shape[-2:], (TILE, 128)))
    block = (1,) * (a.ndim - 2) + tile
    return pl.BlockSpec(block, lambda i: (0,) * a.ndim)


def rim_body(x_ref, b_ref, c_ref, rim_ref):
    rim_ref[:, :WIDE] = x_ref[TILE - RIM :, :]
    rim_ref[:, WIDE : WIDE + G * N] = b_ref[TILE - RIM :, :]
    rim_ref[:, WIDE + G * N :] = c_ref[TILE - RIM :, :]


def rim_rows(x, b, c):
    at = x.shape[0] // TILE - 1
    width = x.shape[1] + b.shape[1] + c.shape[1]
    return pl.pallas_call(
        rim_body,
        grid=(1,),
        in_specs=[pl.BlockSpec((TILE, a.shape[1]), lambda i: (at, 0)) for a in (x, b, c)],
        out_specs=pl.BlockSpec((RIM, width), lambda i: (0, 0)),
        out_shape=jax.ShapeDtypeStruct((RIM, width), BF16),
        compiler_params=params(),
        cost_estimate=cost(1.0),
        name="rim_rows",
    )(*[pltpu.with_memory_space_constraint(a, pltpu.HBM) for a in (x, b, c)])


def whole(a):
    return pl.BlockSpec(a.shape, lambda i: (0,) * len(a.shape))


def split(value, parts):
    found = []
    for _ in range(parts):
        found.append(value.astype(BF16))
        value = value - found[-1].astype(F32)
    groups = []
    for group in range(G):
        lo = group * HEADS
        groups.append(jnp.concatenate([a[:, lo : lo + HEADS] for a in found], axis=1))
    return groups


def spreader(parts):
    head = lax.broadcasted_iota(jnp.int32, (parts * HEADS, COLS), 0) % HEADS
    col = lax.broadcasted_iota(jnp.int32, (parts * HEADS, COLS), 1) // P_SIZE
    return jnp.where(head == col, 1.0, 0.0).astype(BF16)


def by_column(value, matrix, parts):
    rows = jnp.concatenate(split(value, parts), axis=0)
    return jnp.dot(rows, matrix, preferred_element_type=F32)


def steps_body(
    dt_ref,
    decay_ref,
    skip_ref,
    cols_ref,
    rows_ref,
    to_end_ref,
    from_start_ref,
    last_ref,
    skip_cols_ref,
    spread_ref,
):
    raw = dt_ref[...].astype(F32)
    dt = jnp.maximum(raw, 0.0) + jnp.log1p(jnp.exp(-jnp.abs(raw)))
    step = dt * (-jnp.exp(decay_ref[...]))
    row = lax.broadcasted_iota(jnp.int32, (SPAN, SPAN), 0)
    col = lax.broadcasted_iota(jnp.int32, (SPAN, SPAN), 1)
    tri = jnp.where(row >= col, 1.0, 0.0).astype(F32)
    cum = jnp.dot(tri, step, precision=lax.Precision.HIGHEST, preferred_element_type=F32)
    last = cum[SPAN - 1 :, :]
    last_ref[...] = last
    rows_ref[...] = jnp.transpose((cum - jnp.log(dt)) * LOG2E)
    to_end = split(jnp.exp(last - cum) * dt, 2)
    from_start = split(jnp.exp(cum), 2)
    scaled = cum * LOG2E
    for group in range(G):
        lo = group * HEADS
        cols_ref[group] = scaled[:, lo : lo + HEADS]
        to_end_ref[group] = to_end[group]
        from_start_ref[group] = from_start[group]
    skip_cols = by_column(skip_ref[...], spreader(3), 3)
    for group in range(G):
        skip_cols_ref[group] = skip_cols[group : group + 1]
    spread_ref[...] = spreader(2)


def time_steps(dt_input, decay_log, skip_weight):
    given = (dt_input, decay_log.reshape(1, H), skip_weight.reshape(1, H))
    out = [
        jax.ShapeDtypeStruct((G, SPAN, HEADS), F32),
        jax.ShapeDtypeStruct((H, SPAN), F32),
        jax.ShapeDtypeStruct((G, SPAN, 2 * HEADS), BF16),
        jax.ShapeDtypeStruct((G, SPAN, 2 * HEADS), BF16),
        jax.ShapeDtypeStruct((1, H), F32),
        jax.ShapeDtypeStruct((G, 1, COLS), F32),
        jax.ShapeDtypeStruct((2 * HEADS, COLS), BF16),
    ]
    return pl.pallas_call(
        steps_body,
        grid=(1,),
        in_specs=[whole(a) for a in given],
        out_specs=[whole(a) for a in out],
        out_shape=out,
        compiler_params=params(),
        cost_estimate=cost(2.0),
        name="time_steps",
    )(*given)


def convolved(now, rim, kernel, scratch):
    kernel = kernel.astype(F32) * 0.5
    tokens = now.shape[0]
    now = now.astype(F32)
    scratch[PAD - RIM : PAD, :] = rim.astype(F32)
    scratch[PAD : PAD + tokens, :] = now
    half = kernel[RIM : RIM + 1] * now
    for tap in range(RIM):
        first = PAD - RIM + tap
        half = half + kernel[tap : tap + 1] * scratch[first : first + tokens, :]
    return (half + half * jnp.tanh(half)).astype(BF16)


def give_state(state, at, flag_ref, last_ref, keep_ref, send_ref):
    upper = flag_ref[:1] > 0.5
    rows = pl.ds(pl.multiple_of(at * HALF, HALF), HALF)
    keep_ref[rows, :] = jnp.where(upper, state[HALF:], state[:HALF])
    send_ref[rows, :] = jnp.where(upper, state[:HALF], state[HALF:])
    if send_ref.shape[0] > keep_ref.shape[0]:
        put_log(send_ref, keep_ref.shape[0], last_ref[...])


def states_body(skipped, given, outs, scratch):
    x_ref, b_ref, c_ref, kernel_x_ref, kernel_b_ref, kernel_c_ref, to_end_ref, spread_ref = given[:8]
    values_ref, conv_b_ref, conv_c_ref = outs[:3]
    rims = given[8:11] if not skipped else [None] * 3
    tokens = x_ref.shape[0]

    def conv(ref, rim_ref, kernel_ref, lo, turn):
        sl = slice(lo, lo + 128)
        rim = jnp.zeros((RIM, 128), F32) if rim_ref is None else rim_ref[:, sl]
        return convolved(ref[:, sl], rim, kernel_ref[:, sl], scratch.at[turn])

    conv_b = conv(b_ref, rims[1], kernel_b_ref, 0, 0)
    conv_b_ref[...] = conv_b
    conv_c_ref[...] = conv(c_ref, rims[2], kernel_c_ref, 0, 1)
    gain = jnp.dot(to_end_ref[0], spread_ref[...], preferred_element_type=F32)
    weighted = []
    for at in range(x_ref.shape[1] // 128):
        sl = slice(at * 128, (at + 1) * 128)
        part = conv(x_ref, rims[0], kernel_x_ref, at * 128, at % 2)
        values_ref[:, sl] = part
        weighted.append((part.astype(F32) * gain[:, sl]).astype(BF16))
    weighted = jnp.concatenate(weighted, axis=1)
    return lax.dot_general(
        conv_b[skipped:tokens],
        weighted[skipped:tokens],
        (((0,), (0,)), ((), ())),
        preferred_element_type=F32,
    )


B_AT, C_AT = H * P_SIZE // N, H * P_SIZE // N + G


def conv_specs(first, tokens):
    def cols(offset):
        return lambda i: (0, offset + first + i)

    return [
        pl.BlockSpec((tokens, COLS), cols(0)),
        pl.BlockSpec((tokens, N), cols(0)),
        pl.BlockSpec((tokens, N), cols(0)),
        pl.BlockSpec((KERNEL_TAPS, COLS), cols(0)),
        pl.BlockSpec((KERNEL_TAPS, N), cols(B_AT)),
        pl.BlockSpec((KERNEL_TAPS, N), cols(C_AT)),
        pl.BlockSpec((1, tokens, 2 * HEADS), lambda i: (first + i, 0, 0)),
        pl.BlockSpec((2 * HEADS, COLS), lambda i: (0, 0)),
    ]


def rim_specs(first):
    def cols(offset):
        return lambda i: (0, offset + first + i)

    return [
        pl.BlockSpec((RIM, COLS), cols(0)),
        pl.BlockSpec((RIM, N), cols(B_AT)),
        pl.BlockSpec((RIM, N), cols(C_AT)),
    ]


def value_specs(tokens):
    return [pl.BlockSpec((tokens, width), lambda i: (0, i)) for width in (COLS, N, N)]


def value_shapes(count):
    return [jax.ShapeDtypeStruct((SPAN, count * width), BF16) for width in (COLS, N, N)]


def state_outs(first, count):
    rows = count * HALF
    shapes = [(rows, COLS), (rows + log_rows(first), COLS)]
    shapes = [jax.ShapeDtypeStruct(a, BF16) for a in shapes]
    return shapes + [mark()], [whole(a) for a in shapes] + [MARK]


def early_states(first, count, x, b, c, conv_weight, to_end, spread, after):
    def body(*refs):
        outs = refs[8 + len(after) :]
        outs[3][0] = states_body(TILE, refs[:8], outs, outs[-1])
        outs[4][...] = jnp.zeros_like(outs[4])

    return pl.pallas_call(
        body,
        grid=(count,),
        in_specs=conv_specs(first, SPAN) + [corner(a) for a in after],
        out_specs=value_specs(SPAN) + [pl.BlockSpec((1, N, COLS), lambda i: (i, 0, 0)), MARK],
        out_shape=value_shapes(count)
        + [jax.ShapeDtypeStruct((count, N, COLS), F32), mark()],
        scratch_shapes=[pltpu.VMEM((2, PAD + SPAN, 128), F32)],
        compiler_params=params(),
        cost_estimate=cost(1.0),
        name="early_states",
    )(x, b, c, conv_weight, conv_weight, conv_weight, to_end, spread, *after)


def late_states(first, count, early, x, b, c, rim, conv_weight, to_end, spread, flags, last, us):
    values, conv_b, conv_c, partial, token = early

    def body(*refs):
        flag_ref, last_ref, partial_ref = refs[11:14]
        outs = refs[18:]
        state = states_body(0, refs[:11], outs, outs[-1]) + partial_ref[0]
        give_state(state.astype(BF16), pl.program_id(0), flag_ref, last_ref, *outs[3:5])
        outs[5][...] = jnp.zeros_like(outs[5])

    shapes, specs = state_outs(first, count)
    return pl.pallas_call(
        body,
        grid=(count,),
        in_specs=conv_specs(first, TILE)
        + rim_specs(first)
        + [whole(flags), whole(last), pl.BlockSpec((1, N, COLS), lambda i: (i, 0, 0))]
        + [pl.BlockSpec(memory_space=pl.ANY)] * 3
        + [corner(token)],
        out_specs=value_specs(TILE) + specs,
        out_shape=value_shapes(count) + shapes,
        input_output_aliases={14: 0, 15: 1, 16: 2},
        scratch_shapes=[pltpu.VMEM((2, PAD + SPAN, 128), F32)],
        compiler_params=params(),
        cost_estimate=cost(us),
        name="late_states",
    )(
        x, b, c, conv_weight, conv_weight, conv_weight, to_end, spread, rim, rim, rim,
        flags, last, partial, values, conv_b, conv_c, token,
    )


def end_states(first, count, x, b, c, rim, conv_weight, to_end, spread, flags, last, after, us=1.0):
    def body(*refs):
        outs = refs[13 + len(after) :]
        state = states_body(0, refs[:11], outs, outs[-1])
        give_state(state.astype(BF16), pl.program_id(0), *refs[11:13], *outs[3:5])
        outs[5][...] = jnp.zeros_like(outs[5])

    shapes, specs = state_outs(first, count)
    return pl.pallas_call(
        body,
        grid=(count,),
        in_specs=conv_specs(first, SPAN)
        + rim_specs(first)
        + [whole(flags), whole(last)]
        + [corner(a) for a in after],
        out_specs=value_specs(SPAN) + specs,
        out_shape=value_shapes(count) + shapes,
        scratch_shapes=[pltpu.VMEM((2, PAD + SPAN, 128), F32)],
        compiler_params=params(),
        cost_estimate=cost(us),
        name="end_states",
    )(
        x, b, c, conv_weight, conv_weight, conv_weight, to_end, spread, rim, rim, rim,
        flags, last, *after,
    )


def inside_body(values_ref, b_ref, c_ref, cols_ref, rows_ref, skip_ref, part_ref, mark_ref):
    mark_ref[...] = jnp.zeros_like(mark_ref)
    half = SPAN // 2
    scores = lax.dot_general(
        c_ref[...], b_ref[...], (((1,), (1,)), ((), ())), preferred_element_type=F32
    )
    row = lax.broadcasted_iota(jnp.int32, (half, half), 0)
    col = lax.broadcasted_iota(jnp.int32, (half, half), 1)
    causal = row >= col
    lane = lax.broadcasted_iota(jnp.int32, (half, 2 * P_SIZE), 1)
    first_head = lane < P_SIZE
    cols = cols_ref[0]
    rows = rows_ref[...]
    corner, below, later = scores[:half, :half], scores[half:, :half], scores[half:, half:]
    for pair in range(HEADS // 2):
        upper, lower = [], []
        for head in (2 * pair, 2 * pair + 1):
            at_t = cols[:, head : head + 1]
            at_s = rows[head : head + 1, :]
            e = jnp.exp2(at_t[:half] - at_s[:, :half])
            upper.append(jnp.where(causal, corner * e, 0.0).astype(BF16))
            e = jnp.exp2(at_t[half:] - at_s[:, :half])
            left = (below * e).astype(BF16)
            e = jnp.exp2(at_t[half:] - at_s[:, half:])
            right = jnp.where(causal, later * e, 0.0).astype(BF16)
            lower.append(jnp.concatenate([left, right], axis=1))
        sl = slice(pair * 2 * P_SIZE, (pair + 1) * 2 * P_SIZE)
        values = values_ref[:, sl]
        skip = skip_ref[0, :, sl]
        for lo, mix, depth in ((0, upper, half), (half, lower, SPAN)):
            both = jnp.dot(
                jnp.concatenate(mix, axis=0), values[:depth], preferred_element_type=F32
            )
            inside = jnp.where(first_head, both[:half], both[half:])
            part_ref[lo : lo + half, sl] = inside + skip * values[lo : lo + half].astype(F32)


def inside_block(first, count, values, conv_b, conv_c, cols, rows, skip, after, us=1.0):
    assert first % count == 0
    chunk = first // count

    def body(*refs):
        values_ref, b_ref, c_ref, cols_ref, rows_ref, skip_ref = refs[:6]
        part_ref, mark_ref = refs[6 + len(after) :]
        for at in range(count):
            wide, state = pl.ds(at * COLS, COLS), pl.ds(at * N, N)
            inside_body(
                values_ref.at[:, wide],
                b_ref.at[:, state],
                c_ref.at[:, state],
                cols_ref.at[pl.ds(at, 1)],
                rows_ref.at[pl.ds(at * HEADS, HEADS)],
                skip_ref.at[pl.ds(at, 1)],
                part_ref.at[:, wide],
                mark_ref,
            )

    return pl.pallas_call(
        body,
        grid=(1,),
        in_specs=[
            whole(values),
            whole(conv_b),
            whole(conv_c),
            pl.BlockSpec((count, SPAN, HEADS), lambda i: (chunk, 0, 0)),
            pl.BlockSpec((count * HEADS, SPAN), lambda i: (chunk, 0)),
            pl.BlockSpec((count, 1, COLS), lambda i: (chunk, 0, 0)),
        ]
        + [corner(a) for a in after],
        out_specs=[pl.BlockSpec((SPAN, count * COLS), lambda i: (0, 0)), MARK],
        out_shape=[jax.ShapeDtypeStruct((SPAN, count * COLS), F32), mark()],
        compiler_params=params(),
        cost_estimate=cost(us),
        name="inside_block",
    )(values, conv_b, conv_c, cols, rows, skip, *after)


def carried_body(*refs):
    side_ref, c_ref, part_ref, keep_ref, got_ref, from_start_ref, spread_ref = refs[:7]
    out_ref, mark_ref = refs[-2:]
    mark_ref[...] = jnp.zeros_like(mark_ref)
    upper = side_ref[:1] > 0.5
    keep, got = keep_ref[...], got_ref[...]
    carry = jnp.concatenate(
        [jnp.where(upper, got, keep), jnp.where(upper, keep, got)], axis=0
    )
    gain = jnp.dot(from_start_ref[0], spread_ref[...], preferred_element_type=F32)
    carried = jnp.dot(c_ref[...], carry, preferred_element_type=F32)
    out_ref[...] = (part_ref[...] + carried * gain).astype(BF16)


def with_carry(first, count, side, conv_c, part, keep, got, from_start, spread, out, after, us=1.0):
    def own(i):
        return (0, i)

    given = [] if out is None else [out]
    return pl.pallas_call(
        carried_body,
        grid=(count,),
        in_specs=[
            whole(side),
            pl.BlockSpec((SPAN, N), own),
            pl.BlockSpec((SPAN, COLS), own),
            pl.BlockSpec((HALF, COLS), lambda i: (i, 0)),
            pl.BlockSpec((HALF, COLS), lambda i: (i, 0)),
            pl.BlockSpec((1, SPAN, 2 * HEADS), lambda i: (first + i, 0, 0)),
            pl.BlockSpec((2 * HEADS, COLS), lambda i: (0, 0)),
        ]
        + [pl.BlockSpec(memory_space=pl.ANY)] * len(given)
        + [corner(a) for a in after],
        out_specs=[pl.BlockSpec((SPAN, COLS), lambda i: (0, first + i)), MARK],
        out_shape=[jax.ShapeDtypeStruct((SPAN, WIDE), BF16), mark()],
        input_output_aliases={7: 0} if given else {},
        compiler_params=params(),
        cost_estimate=cost(us),
        name="with_carry",
    )(side, conv_c, part, keep, got, from_start, spread, *given, *after)


def swap(value, axis, pairs):
    return lax.ppermute(value, axis, pairs + [(b, a) for a, b in pairs])


def log_rows(first):
    return TILE if first == 0 else 0


def put_log(ref, at, log):
    ref[at:, :] = jnp.zeros((TILE, COLS), BF16)
    parts = []
    for _ in range(3):
        parts.append(log.astype(BF16).astype(F32))
        log = log - parts[-1]
    rest = jnp.zeros((TILE - len(parts), H), F32)
    ref[at:, :H] = jnp.concatenate(parts + [rest], axis=0).astype(BF16)


def take_log(ref, at):
    rows = ref[at:, :H].astype(F32)
    return rows[0:1] + rows[1:2] + rows[2:3]


Y_PAIRS = [(0, 1), (2, 3), (4, 5), (6, 7)]
Z_PAIRS = [(0, 2), (1, 3), (4, 6), (5, 7)]
MID_PAIRS = [(2, 4), (3, 5)]
FAR_PAIRS = [(0, 4), (1, 5), (2, 6), (3, 7)]

ORDER = (
    [("early", 0, 1.0), ("state", 0, 1.0), ("state", 1, 1.0), ("state", 2, 1.0), ("chip", 0, 1.0)]
    + [("state", 3, 1.0), ("chip", 1, 1.0), ("chips", 0, 1.0), ("chip", 2, 1.0)]
    + [("chips", 1, 1.0), ("chip", 3, 1.0), ("inside", 0, 1.0), ("link", 0, 1.0)]
    + [("chips", 2, 1.0), ("link", 1, 1.0), ("chips", 3, 1.0), ("inside", 1, 1.0)]
    + [("total", 0, 1.0), ("link", 2, 1.0), ("link", 3, 1.0), ("total", 1, 1.0)]
    + [("leave", 0, 1.0), ("total", 2, 1.0), ("leave", 1, 1.0), ("out", 0, 1.0)]
    + [("total", 3, 1.0), ("leave", 2, 1.0), ("out", 1, 1.0), ("leave", 3, 1.0)]
    + [("inside", 2, 1.0), ("inside", 3, 1.0), ("out", 2, 1.0), ("out", 3, 1.0)]
)


def places():
    at, core = lax.axis_index("inner"), lax.axis_index("outer")
    z = at >> 1
    row = lax.broadcasted_iota(jnp.int32, (8, COLS), 0)
    flags = jnp.zeros((8, COLS), F32)
    for number, flag in enumerate(((at & 1) == 1, (z & 1) == 1, z >= 2, core == 1)):
        flags = jnp.where((row == number) & flag, 1.0, flags)
    return flags


def merge(body, arrays, weights, lead, flags, spread, after, outs, us):
    count = min(a.shape[0] for a in arrays) // HALF
    rows = count * HALF
    given = [flags, *arrays]
    out = [jax.ShapeDtypeStruct((rows, COLS), BF16)] * outs
    given += weights
    if lead is not None:
        step, known, used, keeps, sends = lead
        asked = [(n, own or at > 0) for own in used for at, n in enumerate(CHUNKS)]
        given += [spread, known]
        if sends:
            out = [jax.ShapeDtypeStruct((rows + TILE, COLS), BF16)]
        out += [jax.ShapeDtypeStruct((8, H), F32)] * keeps
        out += [jax.ShapeDtypeStruct((n, 1, COLS), F32) for n, given_out in asked if given_out]
    out.append(mark())

    def run(*refs):
        ins = refs[1 : 1 + len(arrays)]
        scale_refs = refs[1 + len(arrays) : 1 + len(arrays) + len(weights)]
        rest = refs[1 + len(arrays) + len(weights) : len(given)]
        results = refs[len(given) + len(after) :]
        on = [refs[0][at : at + 1] > 0.5 for at in range(4)]
        results[-1][...] = jnp.zeros((8, 128), F32)
        scales = [[r[at] for r in scale_refs] for at in range(count)]
        if lead is not None:
            logs = [take_log(r, rows) if r.shape[0] > rows else None for r in ins]
            found, kept, onward = step([a[:, :H] for a in on], logs, rest[1][...])
            if keeps:
                empty = jnp.zeros((8 - len(kept), H), F32)
                results[outs][...] = jnp.concatenate(kept + [empty], axis=0)
            if sends:
                put_log(results[0], rows, onward)
            found = [by_column(row, rest[0][...], 2) for row in found]
            scales = [[f[at : at + 1] for f in found] + scales[at] for at in range(count)]
            at = outs + keeps
            first = 0
            for number, (n, given_out) in enumerate(asked):
                value = found[number // len(CHUNKS)]
                first = 0 if number % len(CHUNKS) == 0 else first
                if given_out:
                    for group in range(n):
                        results[at][group] = value[first + group : first + group + 1]
                    at += 1
                first += n
        for at in range(count):
            part = slice(at * HALF, (at + 1) * HALF)
            values = body(on, [r[part, :].astype(F32) for r in ins], scales[at])
            for ref, value in zip(results, values):
                ref[part, :] = value.astype(BF16)

    found = pl.pallas_call(
        run,
        grid=(1,),
        in_specs=[whole(a) for a in given] + [corner(a) for a in after],
        out_specs=[whole(a) for a in out],
        out_shape=out,
        compiler_params=params(),
        cost_estimate=cost(us),
        name=body.__name__,
    )(*given, *after)
    if lead is None:
        return found[:outs], found[-1], None, None
    new = list(found[outs + keeps : -1])
    scales = [new.pop(0) if given_out else None for _, given_out in asked]
    n = len(CHUNKS)
    scales = [scales[n * at : n * (at + 1)] for at in range(len(used))]
    return found[:outs], found[-1], found[outs] if keeps else None, scales


def add_chip(on, arrays, scales):
    upper, _, _, _ = on
    keep, got = arrays
    return (jnp.where(upper, got, keep) * scales[0] + jnp.where(upper, keep, got),)


def chip_logs(on, logs, known):
    upper, _, _, _ = on
    own, got = known[0:1], logs[1]
    low, high = jnp.where(upper, got, own), jnp.where(upper, own, got)
    return [jnp.exp(high), jnp.exp(low)], [low + high], low + high


def add_chips(on, arrays, scales):
    _, odd, _, _ = on
    chip, got = arrays
    return (jnp.where(odd, got, chip) * scales[0] + jnp.where(odd, chip, got),)


def chips_logs(on, logs, known):
    _, odd, _, _ = on
    own, got = known[0:1], logs[1]
    low, high = jnp.where(odd, got, own), jnp.where(odd, own, got)
    return [jnp.exp(high), jnp.exp(own)], [low + high, low], low + high


def go_on(on, arrays, scales):
    _, _, high, _ = on
    chip, two, got = arrays
    own, other, through = scales
    return (jnp.where(high, got * through + chip, two * own + got * other),)


def go_on_logs(on, logs, known):
    _, _, high, _ = on
    own, low, got = known[0:1], known[1:2], logs[2]
    none = jnp.zeros_like(own)
    weights = [jnp.exp(jnp.where(high, none, got)), jnp.exp(jnp.where(high, own, none))]
    return weights, [got, low], got


def add_all(on, arrays, scales):
    _, odd, high, _ = on
    chip, two, got, far = arrays
    own, other, through = scales[:3]
    at_end = jnp.where(high, far * through + chip, far)
    return (jnp.where(odd != high, two * own + got * other, at_end),)


def enter_logs(on, logs, known):
    _, odd, high, core = on
    other, low, further = known[0:1], known[1:2], logs[4]
    none = jnp.zeros_like(other)
    below = jnp.where(odd, low, none)
    reach = jnp.where(high, jnp.where(odd, further, other), none) + below
    return [jnp.where(core, jnp.exp(reach), none)], [], None


def enter(on, arrays, scales):
    upper, odd, high, _ = on
    keep, got_y, got_z, got, far, before = arrays
    reach, below = scales
    low_side = jnp.where(odd, got_z, jnp.zeros_like(got_z))
    entering = jnp.where(high, jnp.where(odd, far, got), low_side) + before * reach
    above = entering * below + jnp.where(upper, got_y, keep)
    return jnp.where(upper, above, entering), jnp.where(upper, entering, above)


def in_order(x, b, c, rim, conv_weight, steps, flags):
    cols, rows, to_end, from_start, last, skip, spread = steps
    starts = [sum(CHUNKS[:k]) for k in range(len(CHUNKS))]
    done, weights = {}, {}
    known = last
    after = []
    out = None

    def merged(body, k, names, scales, logs, wanted, outs=1, sends=True):
        nonlocal known
        lead = None
        if k == 0 and logs is not None:
            used = [name not in ("above", "high", "reach") for name in wanted]
            lead = (logs, known, used, int(sends), sends)
        if lead is None:
            scales = wanted + scales
        found, mark, keeps, new = merge(
            body,
            [done[name, k] for name in names],
            [weights[name][k] for name in scales],
            lead,
            flags,
            spread,
            after,
            outs,
            us,
        )
        if lead is not None:
            known = keeps
            weights.update(zip(wanted, new))
        return found, mark

    for what, k, us in ORDER:
        first, count = starts[k], CHUNKS[k]
        if what == "early":
            early = early_states(first, count, x, b, c, conv_weight, to_end, spread, after)
            done["early", k], mark = early, early[-1]
        elif what == "state":
            given = (x, b, c, rim, conv_weight, to_end, spread, flags, last)
            if ("early", k) in done:
                found = late_states(first, count, done["early", k], *given, us)
            else:
                found = end_states(first, count, *given, after, us)
            done["values", k], done["b", k], done["c", k], keep, send, mark = found
            done["keep", k], done["y", k] = keep, swap(send, "inner", Y_PAIRS)
        elif what == "inside":
            given = [done[name, k] for name in ("values", "b", "c")]
            done["inside", k], mark = inside_block(
                first, count, *given, cols, rows, skip, after, us
            )
        elif what == "chip":
            wanted = ["above", "below"]
            if k > 0:
                wanted = ["above"]
            (found,), mark = merged(add_chip, k, ["keep", "y"], [], chip_logs, wanted)
            done["chip", k], done["z", k] = found, swap(found, "inner", Z_PAIRS)
        elif what == "chips":
            wanted = ["high", "through"]
            if k > 0:
                wanted = ["high"]
            (found,), mark = merged(add_chips, k, ["chip", "z"], [], chips_logs, wanted)
            done["chips", k], done["mid", k] = found, swap(found, "inner", MID_PAIRS)
        elif what == "link":
            names = ["chip", "chips", "mid"]
            (found,), mark = merged(
                go_on, k, names, ["through"], go_on_logs, ["own", "other"]
            )
            done["far", k] = swap(found, "inner", Z_PAIRS)
        elif what == "total":
            names = ["chip", "chips", "mid", "far"]
            (found,), mark = merged(
                add_all, k, names, ["own", "other", "through"], None, []
            )
            done["before", k] = swap(found, "outer", [(0, 1)])
        elif what == "leave":
            names = ["keep", "y", "z", "mid", "far", "before"]
            (stay, leave), mark = merged(
                enter, k, names, ["below"], enter_logs, ["reach"], outs=2, sends=False
            )
            done["stay", k], done["back", k] = stay, swap(leave, "inner", Y_PAIRS)
        else:
            given = [done[name, k] for name in ("c", "inside", "stay", "back")]
            out, mark = with_carry(
                first, count, flags, *given, from_start, spread, out, after, us
            )
        after = [mark]
    return out


def combine(earlier, later):
    return (earlier[0] * later[0], later[0][:, None, :] * earlier[1] + later[1])


def enter_by_all_to_all(last, kept, sent):
    size = lax.axis_size("inner")
    upper = (lax.axis_index("inner") & 1) == 1
    wide = 2 * P_SIZE
    pairs = H // 2
    sent = [a[: b.shape[0]] for a, b in zip(sent, kept)]
    keep, send = [jnp.concatenate(a).reshape(G, HALF, COLS) for a in (kept, sent)]
    halves = [jnp.where(upper, send, keep), jnp.where(upper, keep, send)]
    state = jnp.concatenate(halves, axis=1).reshape(G, N, pairs // G, wide)
    state = jnp.swapaxes(state, 1, 2).reshape(pairs, N, wide)
    decay = jnp.repeat(jnp.exp(last[0]), P_SIZE).reshape(pairs, wide)

    def spread(a):
        return lax.all_to_all(a[None], "inner", split_axis=1, concat_axis=0, tiled=True)

    decays, states = spread(decay), spread(state).astype(F32)
    run = (jnp.ones_like(decays[0]), jnp.zeros_like(states[0]))

    def lap(run, item):
        return combine(run, item), run

    total, before = lax.scan(lap, run, (decays, states))
    first = lax.ppermute(total[1].astype(BF16), "outer", [(0, 1)]).astype(F32)
    entering = before[0][:, :, None, :] * first[None] + before[1]
    carry = lax.all_to_all(
        entering.astype(BF16), "inner", split_axis=0, concat_axis=1, tiled=True
    )[0]
    carry = carry.reshape(G, pairs // G, N, wide)
    carry = jnp.swapaxes(carry, 1, 2).reshape(G, N, COLS)
    top, bottom = carry[:, :HALF], carry[:, HALF:]
    stay, got = jnp.where(upper, bottom, top), jnp.where(upper, top, bottom)
    entered = []
    at = 0
    for count in CHUNKS:
        part = [a[at : at + count].reshape(count * HALF, COLS) for a in (stay, got)]
        entered.append(part)
        at += count
    return entered


def one_by_one(x, b, c, rim, conv_weight, steps, flags):
    cols, rows, to_end, from_start, last, skip, spread = steps
    starts = [sum(CHUNKS[:k]) for k in range(len(CHUNKS))]
    states = [
        end_states(
            first, count, x, b, c, rim, conv_weight, to_end, spread, flags, last, []
        )
        for first, count in zip(starts, CHUNKS)
    ]
    entered = enter_by_all_to_all(last, [a[3] for a in states], [a[4] for a in states])
    out = None
    for first, count, state, (keep, got) in zip(starts, CHUNKS, states, entered):
        values, conv_b, conv_c = state[:3]
        part, _ = inside_block(
            first, count, values, conv_b, conv_c, cols, rows, skip, []
        )
        out, _ = with_carry(
            first, count, flags, conv_c, part, keep, got, from_start, spread, out, []
        )
    return out


def shards(x_stream, b_stream, c_stream, dt_input, decay_log, skip_weight, conv_weight):
    devices = lax.axis_size("outer") * lax.axis_size("inner")
    x_stream, dt_input, flags = lax.optimization_barrier((x_stream, dt_input, places()))
    rim = lax.ppermute(
        rim_rows(x_stream, b_stream, c_stream),
        ("outer", "inner"),
        [(i, i + 1) for i in range(devices - 1)],
    )
    steps = time_steps(dt_input, decay_log, skip_weight)
    by_swaps = lax.axis_size("inner") == 8 and lax.axis_size("outer") == 2
    rest = in_order if by_swaps else one_by_one
    return rest(x_stream, b_stream, c_stream, rim, conv_weight, steps, flags)


def solution(mesh):
    return jax.shard_map(
        shards,
        mesh=mesh,
        in_specs=(
            P(("slab", "outer", "inner"), None),
            P(("slab", "outer", "inner"), None),
            P(("slab", "outer", "inner"), None),
            P(("slab", "outer", "inner"), None),
            P("slab"),
            P(),
            P(),
        ),
        out_specs=P(("slab", "outer", "inner"), None),
        check_vma=False,
    )
```
